256 devices in a mesh: region: 64 (over z, y, core), sub: 4 (over x).
Axes of the slice: x: 4, y: 4, z: 8, core: 2. Of those that a mesh axis runs over, the one named last changes fastest.
Arguments:
- innovations: float32 [4096, 16, 128], P(('region', 'sub'))
- ensemble: float32 [4096, 64, 128], P(('region', 'sub')), may hold values from -3 to 3
- coords: int32 [4096, 2, 128], P(('region', 'sub')), may hold values from 0 to 255, as said below
- obs_error: float32 [4096, 128], P(('region', 'sub')), may hold values from 2.5 to 5
- pair_cols: int32 [4096, 9], P(('region', 'sub')), may hold values from 0 to 4095, as said below
- pair_count: int32 [4096], P(('region', 'sub')), may hold values from 1 to 9, as said below
Outputs:
- analysis_weights: float32 [4096, 16, 128], P(('region', 'sub'))
- residual: float32 [4096, 16, 128], P(('region', 'sub'))
The draws below stay inside these ranges and needn't reach their ends.
Inputs may be any that keep to these rules, and one draw needn't show every extreme that they name: `coords`: the first coordinate lies in 0 to 63, the second in 0 to 255. `pair_cols`: the first pair_count[b] entries of row b list, in ascending order, the blocks paired with block b: always b itself, and only blocks c with |c - b| <= 4; c lists b exactly when b lists c. The remaining slots hold b. `pair_count`: the largest value 9 is taken in every draw.
All inputs are finite; a program needn't handle non-finite values.
Results may differ from the reference program's by a relative error of at most 0.00045.
Values sent between devices are 32-bit elements; how exact they have to be, the bound alone decides.
A program may use at most 64 MiB of HBM per device.

```python
import math
import jax
import jax.numpy as jnp
from jax import lax

OBS = 128
RHS = 16
MEM = 64
WMAX = 4
ITERS = 2
BLK_DEV = 16
MAXP = 9
BLOCKS = 4096


def pair_table(key):
    num_blocks = BLOCKS
    devices_all = BLOCKS // BLK_DEV
    level = jax.random.randint(jax.random.fold_in(key, 101), (devices_all,), 1, WMAX + 1)
    spread = jax.random.randint(jax.random.fold_in(key, 102), (num_blocks,), 0, WMAX + 1)
    spread = jnp.minimum(spread, jnp.repeat(level, BLK_DEV))
    anchor = jax.random.randint(jax.random.fold_in(key, 103), (), 0, num_blocks - 2 * WMAX)
    block_ids = jnp.arange(num_blocks, dtype=jnp.int32)
    within = block_ids % BLK_DEV
    at_edge = (within == 0) | (within == BLK_DEV - 1)
    spread = jnp.where(at_edge, jnp.maximum(spread, 1), spread)
    forced = (block_ids >= anchor) & (block_ids <= anchor + 2 * WMAX) | (block_ids < BLK_DEV + WMAX)
    spread = jnp.where(forced, WMAX, spread)
    offsets = jnp.arange(-WMAX, WMAX + 1, dtype=jnp.int32)
    partner = block_ids[:, None] + offsets[None, :]
    inside = (partner >= 0) & (partner < num_blocks)
    partner_spread = spread[jnp.clip(partner, 0, num_blocks - 1)]
    valid = inside & (jnp.abs(offsets)[None, :] <= jnp.minimum(spread[:, None], partner_spread))
    counts = jnp.sum(valid.astype(jnp.int32), axis=1).astype(jnp.int32)
    placed = jnp.cumsum(valid.astype(jnp.int32), axis=1) - 1
    slot_ids = jnp.arange(2 * WMAX + 1, dtype=jnp.int32)
    hits = valid[:, :, None] & (placed[:, :, None] == slot_ids[None, None, :])
    columns = jnp.sum(jnp.where(hits, partner[:, :, None], 0), axis=1)
    columns = jnp.where(slot_ids[None, :] < counts[:, None], columns, block_ids[:, None])
    return (columns.astype(jnp.int32), counts)


def draw_pair_cols(key, part):
    columns, counts = pair_table(key)
    return columns


def draw_pair_count(key, part):
    columns, counts = pair_table(key)
    return counts


def draw_coords(key, part):
    key = jax.random.fold_in(key, 5)
    first_axis = jax.random.randint(jax.random.fold_in(key, 1), (BLOCKS, OBS), 0, 64)
    second_axis = jax.random.randint(jax.random.fold_in(key, 2), (BLOCKS, OBS), 0, 256)
    first_axis = first_axis.at[:, 0].set(0)
    first_axis = first_axis.at[:, 1].set(63)
    second_axis = second_axis.at[:, 0].set(0)
    second_axis = second_axis.at[:, 1].set(255)
    return jnp.stack([first_axis, second_axis], axis=1).astype(jnp.int32)


def draw_innovations(key, part):
    key = jax.random.fold_in(key, 1)
    full_shape = (BLOCKS, RHS, OBS)
    block_ids = jnp.arange(BLOCKS, dtype=jnp.int32)
    position = block_ids.astype(jnp.float32) / max(BLOCKS - 1, 1)
    periods = jnp.array([11, 29, 71], dtype=jnp.int32)
    phase_of_block = (block_ids[:, None] % periods[None, :]).astype(jnp.float32) / periods[None, :].astype(jnp.float32)
    phases = jax.random.uniform(jax.random.fold_in(key, 4), (3, RHS), jnp.float32, 0.0, 6.2831853)
    amplitudes = jax.random.uniform(jax.random.fold_in(key, 5), (3, RHS), jnp.float32, 0.5, 1.0)
    angles = 6.2831853 * phase_of_block[:, :, None] + phases[None, :, :]
    waves = jnp.sum(amplitudes[None, :, :] * jnp.sin(angles), axis=1)
    roughness = jax.random.uniform(jax.random.fold_in(key, 3), (BLOCKS, 1, OBS), jnp.float32, 0.5, 1.5)
    baseline = 0.7 * jax.random.normal(key, full_shape, jnp.float32)
    smooth = 1.2 * waves
    growth = 3.0 ** position
    return (smooth[:, :, None] + baseline * roughness) * growth[:, None, None]


def steps_of(stream_key, extent, shards, least, top_value):
    loudness = 1.0
    for dim, shards_of in shards:
        heights = jax.random.uniform(jax.random.fold_in(jax.random.fold_in(stream_key, 6), dim), (shards_of,), jnp.float32, least / len(shards), top_value / len(shards))
        loudness = loudness * jnp.repeat(jnp.exp(heights), extent[dim] // shards_of).reshape((-1,) + (1,) * (len(extent) - 1 - dim))
    return loudness


def scatter_about(own_key, shape, width, bound, split=(), held_as=jnp.bfloat16):
    gain = steps_of(own_key, shape, split, -0.22, 0.18) if split else 1.0
    values = jax.random.normal(own_key, shape, jnp.float32) * width * gain
    return jnp.minimum(jnp.maximum(values, -bound), bound).astype(held_as)


def setup_inputs(seed: int = 0) -> dict:
    seeds = jax.random.split(jax.random.key(seed), 7)
    return {
        "innovations": draw_innovations(jax.random.fold_in(seeds[6], 71), 0),
        "ensemble": scatter_about(seeds[1], (BLOCKS, MEM, OBS), 0.3, 3.0, ((0, 256),), jnp.float32),
        "coords": draw_coords(jax.random.fold_in(seeds[6], 71), 0),
        "obs_error": jnp.clip(jnp.exp(math.log(5.0) - 0.6931472 * jax.random.uniform(seeds[3], (BLOCKS, OBS), jnp.float32) ** steps_of(seeds[3], (BLOCKS, OBS), ((0, 256),), -0.2, 0.2)), 2.5, 5.0),
        "pair_cols": draw_pair_cols(jax.random.fold_in(seeds[6], 71), 0),
        "pair_count": draw_pair_count(jax.random.fold_in(seeds[6], 71), 0),
    }


corr_length = 150.0
loc_length = 200.0
static_var = 0.002
highest = lax.Precision.HIGHEST

def symmetric(matrix):
    return 0.5 * (matrix + matrix.T)

def gram_matrix(former, latter):
    return jnp.einsum('bra,bsa->rs', former, latter, precision=highest)

def combine(vectors, coeffs):
    return jnp.einsum('bsa,sr->bra', vectors, coeffs, precision=highest)

def solve_spd(matrix, target):
    factor = jnp.linalg.cholesky(matrix)
    return jax.scipy.linalg.cho_solve((factor, True), target)

def covariance_apply(vectors, ensemble, positions, obs_error, pair_cols, pair_count):
    num_blocks = vectors.shape[0]
    groups = num_blocks // 16

    def one_block(block_id):
        partners = pair_cols[block_id]
        live_slot = (jnp.arange(MAXP, dtype=jnp.int32) < pair_count[block_id]).astype(jnp.float32)
        own_pos = positions[block_id]
        theirs = positions[partners]
        across = (own_pos[0][None, :, None] - theirs[:, 0][:, None, :]) ** 2 + (own_pos[1][None, :, None] - theirs[:, 1][:, None, :]) ** 2
        static = static_var * jnp.exp(-jnp.sqrt(across) / corr_length)
        shared = jnp.einsum('ma,smc->sac', ensemble[block_id], ensemble[partners], precision=highest) / (MEM - 1)
        kernel = (static + jnp.exp(-across / (2.0 * loc_length ** 2)) * shared) * live_slot[:, None, None]
        summed = jnp.einsum('sac,src->ra', kernel, vectors[partners], precision=highest)
        return summed + obs_error[block_id][None, :] * vectors[block_id]

    def one_group(group_id):
        return jax.vmap(one_block)(group_id * 16 + jnp.arange(16, dtype=jnp.int32))
    result = lax.map(one_group, jnp.arange(groups, dtype=jnp.int32))
    return result.reshape(vectors.shape)

def reference(innovations, ensemble, coords, obs_error, pair_cols, pair_count):
    block_base = (jnp.arange(coords.shape[0], dtype=jnp.int32) * 64).astype(jnp.float32)
    first_only = jnp.array([1.0, 0.0], dtype=jnp.float32)
    positions = coords.astype(jnp.float32) + block_base[:, None, None] * first_only[None, :, None]
    weights = jnp.zeros_like(innovations)
    residual = innovations
    direction = innovations
    res_gram = symmetric(gram_matrix(residual, residual))
    for iteration in range(ITERS):
        applied = covariance_apply(direction, ensemble, positions, obs_error, pair_cols, pair_count)
        step_size = solve_spd(symmetric(gram_matrix(direction, applied)), res_gram)
        weights = weights + combine(direction, step_size)
        residual = residual - combine(applied, step_size)
        if iteration + 1 < ITERS:
            updated = symmetric(gram_matrix(residual, residual))
            mixing = solve_spd(res_gram, updated)
            direction = residual + combine(direction, mixing)
            res_gram = updated
    return (weights, residual)
```

```python
import functools

import jax
import jax.numpy as jnp
import numpy as np
from jax import lax
from jax.experimental import pallas as pl
from jax.experimental.pallas import tpu as pltpu
from jax.sharding import PartitionSpec as P

MESH = pl.DeviceIdType.MESH
F32 = jnp.float32
BF16 = jnp.bfloat16

NB = 16
W = 4
NX = NB + 2 * W
SLOTS = 2 * W + 1
OBS = 128
RHS = 16
MEM = 64
SPAN = SLOTS * OBS

STATIC_VAR = 0.002
LOG2E = 1.4426950408889634
C_CORR = -LOG2E / 150.0
C_LOC = -LOG2E / (2.0 * 200.0**2)
ENS_SCALE = 1.0 / ((MEM - 1) * STATIC_VAR)


def split(value):
    hi = value.astype(BF16)
    lo = (value - hi.astype(F32)).astype(BF16)
    return hi, lo


def rows_of(rows, dtype=F32):
    ids = lax.broadcasted_iota(jnp.int32, (16, OBS), 0)
    out = jnp.zeros((16, OBS), F32)
    for place, row in enumerate(rows):
        out = jnp.where(ids == place, jnp.broadcast_to(row, (16, OBS)), out)
    return out.astype(dtype)


def features(crd, place):
    x = crd[0:1, :].astype(F32)
    y = crd[1:2, :].astype(F32)
    base = (place - NX // 2).astype(F32) * 64.0
    base = jnp.full((1, OBS), base, F32)
    full = x + base
    square = full * full + y * y
    s1 = square.astype(BF16).astype(F32)
    s2 = (square - s1).astype(BF16).astype(F32)
    s3 = square - s1 - s2
    one = jnp.ones((1, OBS), F32)
    left = [s1, s2, s3, one, one, one, base, base, x, x, y]
    right = [one, one, one, s1, s2, s3, -2.0 * base, -2.0 * x, -2.0 * base, -2.0 * x, -2.0 * y]
    return left, right


def kernel(
    innov, ens, coords, obs, cols, w_out, r_out,
    lhsx, rhs, kmat, zx, zf, maskx,
    ens_lo, ens_hi, crd_lo, crd_hi, v_lo, v_hi, p_lo, p_hi,
    part_a, part_b, red_a, red_b,
    halo_send, halo_recv, send_a, recv_a, send_b, recv_b,
):
    me = lax.axis_index("region") * 4 + lax.axis_index("sub")

    def device(index):
        return (lax.div(index, 4), lax.rem(index, 4))

    left = device(lax.rem(me + 255, 256))
    right = device(lax.rem(me + 1, 256))
    x = lax.rem(me, 4)
    core = lax.rem(lax.div(me, 4), 2)
    y = lax.rem(lax.div(me, 8), 4)
    z = lax.div(me, 32)

    def peer_a(step):
        there = lax.rem(y * 4 + x + step, 16)
        return device(((z * 4 + lax.div(there, 4)) * 2 + core) * 4 + lax.rem(there, 4))

    def peer_b(step):
        there = lax.rem(z * 2 + core + step, 16)
        return device(((lax.div(there, 2) * 4 + y) * 2 + lax.rem(there, 2)) * 4 + x)

    barrier = pltpu.get_barrier_semaphore()
    for there in (left, right):
        pl.semaphore_signal(barrier, inc=1, device_id=there, device_id_type=MESH)

    def greet(step, carry):
        pl.semaphore_signal(barrier, inc=1, device_id=peer_a(step), device_id_type=MESH)
        pl.semaphore_signal(barrier, inc=1, device_id=peer_b(step), device_id_type=MESH)
        return carry

    lax.fori_loop(1, 16, greet, 0)
    pl.semaphore_wait(barrier, 32)

    def remote(src, dst, slot, there):
        return pltpu.make_async_remote_copy(
            src_ref=src, dst_ref=dst, send_sem=halo_send.at[slot], recv_sem=halo_recv.at[slot],
            device_id=there, device_id_type=MESH,
        )

    static = [
        remote(ens.at[NB - W : NB], ens_lo, 0, right),
        remote(ens.at[0:W], ens_hi, 1, left),
        remote(coords.at[NB - W : NB], crd_lo, 2, right),
        remote(coords.at[0:W], crd_hi, 3, left),
        remote(innov.at[NB - W : NB], v_lo, 4, right),
        remote(innov.at[0:W], v_hi, 5, left),
    ]
    for copy in static:
        copy.start()

    own = lax.broadcasted_iota(jnp.int32, (NB, SLOTS), 0) + me * NB
    offset = cols[...] - own
    for slot in range(SLOTS):
        hit = jnp.max(jnp.where(offset == slot - W, 1.0, 0.0).astype(F32), axis=1, keepdims=True)
        wide = jnp.broadcast_to(hit, (NB, OBS))
        for b in range(NB):
            maskx[b, :, slot * OBS : (slot + 1) * OBS] = jnp.broadcast_to(wide[b : b + 1, :], (RHS, OBS)).astype(BF16)

    def lanes(place):
        return pl.ds(pl.multiple_of(place * OBS, OBS), OBS)

    def prepare(place, members, crd, vectors):
        hi, lo = split(members)
        feats, weights = features(crd, place)
        stacked = jnp.concatenate(
            [hi, hi, lo, rows_of(feats, BF16), jnp.zeros((48, OBS), BF16)], axis=0
        )
        lhsx[place] = stacked.T
        v_hi_part, v_lo_part = split(vectors)
        zx[0:16, lanes(place)] = v_hi_part
        zx[16:32, lanes(place)] = v_lo_part
        return weights

    def prepare_own(b, carry):
        members = ens[b]
        vectors = innov[b]
        weights = prepare(b + W, members, coords[b], vectors)
        hi, lo = split(members * ENS_SCALE)
        none = jnp.zeros((64, OBS), BF16)
        rhs[b, 0:64, 0:128] = hi
        rhs[b, 64:128, 0:128] = lo
        rhs[b, 128:192, 0:128] = hi
        rhs[b, 192:256, 0:128] = none
        rhs[b, 0:192, 128:256] = jnp.zeros((192, OBS), BF16)
        rhs[b, 192:208, 128:256] = rows_of(weights, BF16)
        rhs[b, 208:256, 128:256] = jnp.zeros((48, OBS), BF16)
        zf[0:16, lanes(b)] = vectors
        return carry

    lax.fori_loop(0, NB, prepare_own, 0)

    def tiles(b):
        weights = rhs[b]
        for slot in range(SLOTS):
            both = jnp.dot(lhsx[b + slot], weights, preferred_element_type=F32)
            shared = both[:, 0:128]
            square = both[:, 128:256]
            inverse = lax.rsqrt(jnp.maximum(square, 1e-30))
            value = jnp.exp2(square * C_CORR * inverse) + jnp.exp2(square * C_LOC) * shared
            hi, lo = split(value)
            kmat[b, slot * OBS : (slot + 1) * OBS, 0:128] = hi
            kmat[b, slot * OBS : (slot + 1) * OBS, 128:256] = lo

    def apply(b, row, out_row, vec):
        window = pl.ds(pl.multiple_of(b * OBS, OBS), SPAN)
        mask = maskx[b]
        vectors = jnp.concatenate([zx[row : row + 16, window] * mask, zx[row + 16 : row + 32, window] * mask], axis=0)
        part = jnp.dot(vectors, kmat[b], preferred_element_type=F32)
        part = part[0:16] + part[16:32]
        total = (part[:, 0:128] + part[:, 128:256]) * STATIC_VAR + obs[pl.ds(b, 1), :] * vec
        zf[out_row : out_row + 16, lanes(b)] = total
        hi, lo = split(total)
        zx[row + 32 : row + 48, lanes(b + W)] = hi
        zx[row + 48 : row + 64, lanes(b + W)] = lo

    def first(b, carry):
        tiles(b)
        apply(b, 0, 16, zf[0:16, lanes(b)])
        return carry

    def second(b, carry):
        apply(b, 32, 32, zf[16:32, lanes(b)])
        return carry

    lax.fori_loop(W, NB - W, first, 0)
    for copy in static:
        copy.wait()

    def prepare_halo(i, carry):
        prepare(i, ens_lo[i], crd_lo[i], v_lo[i])
        prepare(i + NB + W, ens_hi[i], crd_hi[i], v_hi[i])
        return carry

    lax.fori_loop(0, W, prepare_halo, 0)
    lax.fori_loop(0, W, first, 0)
    lax.fori_loop(NB - W, NB, first, 0)

    moving = [
        remote(zf.at[16:32, (NB - W) * OBS : NB * OBS], p_lo, 6, right),
        remote(zf.at[16:32, 0 : W * OBS], p_hi, 7, left),
    ]
    for copy in moving:
        copy.start()
    lax.fori_loop(W, NB - W, second, 0)
    for copy in moving:
        copy.wait()
    for source, start in ((p_lo, 0), (p_hi, (NB + W) * OBS)):
        hi, lo = split(source[...])
        zx[32:48, start : start + W * OBS] = hi
        zx[48:64, start : start + W * OBS] = lo
    lax.fori_loop(0, W, second, 0)
    lax.fori_loop(NB - W, NB, second, 0)

    inner = slice(W * OBS, (W + NB) * OBS)
    gram = lax.dot_general(
        zx[0:64, inner], zx[0:96, inner], (((1,), (1,)), ((), ())), preferred_element_type=F32
    )
    gram = jnp.concatenate([gram, jnp.zeros((64, 32), F32)], axis=1)
    lane = lax.broadcasted_iota(jnp.int32, (16, OBS), 1)
    lane8 = lax.broadcasted_iota(jnp.int32, (8, OBS), 1)

    def turn(value, by):
        return pltpu.roll(value, by % OBS, 1)

    of_r = gram[0:16] + gram[16:32]
    of_p = gram[32:48] + gram[48:64]
    of_r = of_r + turn(of_r, -16)
    of_p = of_p + turn(of_p, -16)
    even = (lane & 16) == 0
    own_part = jnp.where(even, of_r, turn(of_p, -16))
    part_a[...] = jnp.where(lane8 < 64, own_part[0:8], turn(own_part[8:16], 64))

    def exchange(part, red, peer, send, recv):
        def copy(step):
            return pltpu.make_async_remote_copy(
                src_ref=part, dst_ref=red.at[step - 1], send_sem=send.at[step - 1], recv_sem=recv.at[step - 1],
                device_id=peer(step), device_id_type=MESH,
            )

        def start(step, carry):
            copy(step).start()
            return carry

        def wait(step, carry):
            copy(step).wait()
            return carry

        lax.fori_loop(1, 16, start, 0)
        lax.fori_loop(1, 16, wait, 0)
        return part[...] + jnp.sum(red[...], axis=0)

    part_b[...] = exchange(part_a, red_a, peer_a, send_a, recv_a)
    packed = exchange(part_b, red_b, peer_b, send_b, recv_b)

    moments = jnp.concatenate([packed, turn(packed, 64)], axis=0)
    top = jnp.where(lane < 16, turn(moments, -32), jnp.where(lane < 32, moments, turn(moments, 32)))
    low = jnp.where(lane < 16, turn(moments, -16), jnp.where(lane < 32, turn(moments, -32), moments))
    system = jnp.concatenate([top, low], axis=0)
    rows = lax.broadcasted_iota(jnp.int32, (32, OBS), 0)
    for k in range(32):
        pivot = 1.0 / system[k : k + 1, k : k + 1]
        row = system[k : k + 1, :] * pivot
        system = jnp.where(rows == k, row, system - system[:, k : k + 1] * row)

    solved = jnp.concatenate([system, jnp.zeros((96, OBS), F32)], axis=0).T
    coeffs = solved[32:48, :]
    zero = jnp.zeros((16, OBS), F32)
    for_w = jnp.where(lane < 32, coeffs, zero)
    for_r = turn(for_w, 16)
    both = jnp.concatenate([for_w, for_r], axis=0)[:, 0:48]
    for chunk in range(4):
        out = jnp.dot(
            both, zf[:, chunk * 512 : (chunk + 1) * 512], preferred_element_type=F32, precision=lax.Precision.HIGHEST
        )
        for piece in range(4):
            b = chunk * 4 + piece
            here = out[:, piece * OBS : (piece + 1) * OBS]
            w_out[b] = here[0:16]
            r_out[b] = innov[b] - here[16:32]


def on_device(innovations, ensemble, coords, obs_error, pair_cols, pair_count):
    del pair_count
    vmem = pl.BlockSpec(memory_space=pltpu.VMEM)
    out = jax.ShapeDtypeStruct((NB, RHS, OBS), F32)
    return pl.pallas_call(
        kernel,
        out_shape=(out, out),
        in_specs=[vmem] * 5,
        out_specs=(vmem, vmem),
        scratch_shapes=[
            pltpu.VMEM((NX, OBS, 256), BF16),
            pltpu.VMEM((NB, 256, 256), BF16),
            pltpu.VMEM((NB, SPAN, 256), BF16),
            pltpu.VMEM((96, NX * OBS), BF16),
            pltpu.VMEM((48, NB * OBS), F32),
            pltpu.VMEM((NB, RHS, SPAN), BF16),
            pltpu.VMEM((W, MEM, OBS), F32),
            pltpu.VMEM((W, MEM, OBS), F32),
            pltpu.VMEM((W, 2, OBS), jnp.int32),
            pltpu.VMEM((W, 2, OBS), jnp.int32),
            pltpu.VMEM((W, RHS, OBS), F32),
            pltpu.VMEM((W, RHS, OBS), F32),
            pltpu.VMEM((RHS, W * OBS), F32),
            pltpu.VMEM((RHS, W * OBS), F32),
            pltpu.VMEM((8, OBS), F32),
            pltpu.VMEM((8, OBS), F32),
            pltpu.VMEM((15, 8, OBS), F32),
            pltpu.VMEM((15, 8, OBS), F32),
            pltpu.SemaphoreType.DMA((8,)),
            pltpu.SemaphoreType.DMA((8,)),
            pltpu.SemaphoreType.DMA((15,)),
            pltpu.SemaphoreType.DMA((15,)),
            pltpu.SemaphoreType.DMA((15,)),
            pltpu.SemaphoreType.DMA((15,)),
        ],
        compiler_params=pltpu.CompilerParams(
            collective_id=0, has_side_effects=True, vmem_limit_bytes=48 * 1024 * 1024
        ),
    )(innovations, ensemble, coords, obs_error, pair_cols)


def solution(mesh):
    both = ("region", "sub")
    in_specs = (
        P(both, None, None),
        P(both, None, None),
        P(both, None, None),
        P(both, None),
        P(both, None),
        P(both),
    )
    out_specs = (P(both, None, None), P(both, None, None))
    return jax.shard_map(on_device, mesh=mesh, in_specs=in_specs, out_specs=out_specs, check_vma=False)
```

```python
import jax
import jax.numpy as jnp
from jax import lax
from jax.experimental import pallas as pl
from jax.experimental.pallas import tpu as pltpu
from jax.sharding import PartitionSpec as P

MESH = pl.DeviceIdType.MESH
F32 = jnp.float32
BF16 = jnp.bfloat16

NB = 16
W = 4
NX = NB + 2 * W
SLOTS = 2 * W + 1
HALF = W + 1
OBS = 128
RHS = 16
MEM = 64

STATIC_VAR = 0.002
LOG2E = 1.4426950408889634
C_CORR = -LOG2E / 150.0
C_LOC = -LOG2E / (2.0 * 200.0**2)
ENS_SCALE = 1.0 / ((MEM - 1) * STATIC_VAR)


def split(value):
    hi = value.astype(BF16)
    lo = (value - hi.astype(F32)).astype(BF16)
    return hi, lo


def rows_of(rows):
    ids = lax.broadcasted_iota(jnp.int32, (16, OBS), 0)
    out = jnp.zeros((16, OBS), F32)
    for place, row in enumerate(rows):
        out = jnp.where(ids == place, jnp.broadcast_to(row, (16, OBS)), out)
    return out.astype(BF16)


def position_parts(crd, place):
    x = crd[0:1, :].astype(F32)
    y = crd[1:2, :].astype(F32)
    base = jnp.full((1, OBS), jnp.asarray(place - NX // 2).astype(F32) * 64.0, F32)
    full = x + base
    square = full * full + y * y
    s1 = square.astype(BF16).astype(F32)
    s2 = (square - s1).astype(BF16).astype(F32)
    s3 = square - s1 - s2
    return s1, s2, s3, base, x, y


def kernel(
    innov, ens, coords, obs, cols, out,
    ens_v, crd_v, v_v, obs_v, cols_v,
    lhsx, rhs, kmat, zx, zf, maskx,
    ens_lo, ens_hi, crd_lo, crd_hi, v_lo, v_hi, p_lo, p_hi,
    part_a, part_b, red_a, red_b,
    load_sem, halo_send, halo_recv, send_a, recv_a, send_b, recv_b,
):
    me = lax.axis_index("region") * 4 + lax.axis_index("sub")

    def device(index):
        return (lax.div(index, 4), lax.rem(index, 4))

    left = device(lax.rem(me + 255, 256))
    right = device(lax.rem(me + 1, 256))
    x = lax.rem(me, 4)
    core = lax.rem(lax.div(me, 4), 2)
    y = lax.rem(lax.div(me, 8), 4)
    z = lax.div(me, 32)

    def peer_a(step):
        there = lax.rem(y * 4 + x + step, 16)
        return device(((z * 4 + lax.div(there, 4)) * 2 + core) * 4 + lax.rem(there, 4))

    def peer_b(step):
        there = lax.rem(z * 2 + core + step, 16)
        return device(((lax.div(there, 2) * 4 + y) * 2 + lax.rem(there, 2)) * 4 + x)

    barrier = pltpu.get_barrier_semaphore()
    for there in (left, right):
        pl.semaphore_signal(barrier, inc=1, device_id=there, device_id_type=MESH)

    def greet(step, carry):
        pl.semaphore_signal(barrier, inc=1, device_id=peer_a(step), device_id_type=MESH)
        pl.semaphore_signal(barrier, inc=1, device_id=peer_b(step), device_id_type=MESH)
        return carry

    lax.fori_loop(1, 16, greet, 0)
    loads = [
        pltpu.make_async_copy(source, target, load_sem.at[i])
        for i, (source, target) in enumerate(
            ((cols, cols_v), (coords, crd_v), (ens, ens_v), (innov, v_v), (obs, obs_v))
        )
    ]
    for load in loads:
        load.start()
    pl.semaphore_wait(barrier, 32)

    def remote(src, dst, slot, there):
        return pltpu.make_async_remote_copy(
            src_ref=src, dst_ref=dst, send_sem=halo_send.at[slot], recv_sem=halo_recv.at[slot],
            device_id=there, device_id_type=MESH,
        )

    static = [
        remote(ens.at[NB - W : NB], ens_lo, 0, right),
        remote(ens.at[0:W], ens_hi, 1, left),
        remote(coords.at[NB - W : NB], crd_lo, 2, right),
        remote(coords.at[0:W], crd_hi, 3, left),
        remote(innov.at[NB - W : NB], v_lo, 4, right),
        remote(innov.at[0:W], v_hi, 5, left),
    ]
    for copy in static:
        copy.start()
    for load in loads:
        load.wait()

    offset = cols_v[...] - (lax.broadcasted_iota(jnp.int32, (NB, SLOTS), 0) + me * NB)
    for slot in range(SLOTS):
        hit = jnp.max(jnp.where(offset == slot - W, 1.0, 0.0).astype(F32), axis=1, keepdims=True)
        maskx[slot] = jnp.broadcast_to(hit, (NB, OBS))

    def lanes(place, count=1):
        return pl.ds(pl.multiple_of(place * OBS, OBS), count * OBS)

    def set_vectors(place, vectors):
        hi, lo = split(vectors)
        zx[0:16, lanes(place)] = hi
        zx[16:32, lanes(place)] = lo

    def set_left(place, members, crd):
        hi, lo = split(members)
        s1, s2, s3, base, x, y = position_parts(crd, place)
        one = jnp.ones((1, OBS), F32)
        parts = rows_of([s1, s2, s3, one, one, one, base, base, x, x, y])
        stacked = jnp.concatenate([hi, hi, lo, parts, jnp.zeros((48, OBS), BF16)], axis=0)
        lhsx[place - W] = stacked.T

    def set_right(place, members, crd):
        hi, lo = split(members * ENS_SCALE)
        s1, s2, s3, base, x, y = position_parts(crd, place)
        one = jnp.ones((1, OBS), F32)
        parts = rows_of([one, one, one, s1, s2, s3, -2.0 * base, -2.0 * x, -2.0 * base, -2.0 * x, -2.0 * y])
        rhs[place, 0:64, 0:128] = hi
        rhs[place, 64:128, 0:128] = lo
        rhs[place, 128:192, 0:128] = hi
        rhs[place, 192:256, 0:128] = jnp.zeros((64, OBS), BF16)
        rhs[place, 0:192, 128:256] = jnp.zeros((192, OBS), BF16)
        rhs[place, 192:208, 128:256] = parts
        rhs[place, 208:256, 128:256] = jnp.zeros((48, OBS), BF16)

    def prepare_own(i, carry):
        members = ens_v[i]
        vectors = v_v[i]
        set_left(i + W, members, crd_v[i])
        set_right(i + W, members, crd_v[i])
        set_vectors(i + W, vectors)
        zf[0:16, lanes(i)] = vectors
        zf[16:32, lanes(i)] = obs_v[pl.ds(i, 1), :] * vectors
        return carry

    lax.fori_loop(0, NB, prepare_own, 0)

    def tile(b, j, mask):
        both = jnp.dot(lhsx[b + j - W], rhs[b], preferred_element_type=F32)
        shared = both[:, 0:128]
        square = both[:, 128:256]
        inverse = lax.rsqrt(jnp.maximum(square, 1e-30))
        value = jnp.exp2(square * C_CORR * inverse) + jnp.exp2(square * C_LOC) * shared
        hi, lo = split(value * mask)
        kmat[b, j * OBS : (j + 1) * OBS, 0:128] = hi
        kmat[b, j * OBS : (j + 1) * OBS, 128:256] = lo

    def own_mask(b, j):
        return maskx[j + W, pl.ds(b - W, 1), :]

    def add(row, place, count, part):
        part = part[0:16] + part[16:32]
        zf[row : row + 16, lanes(place - W, count)] += part * STATIC_VAR

    def gather(b, start, stop, row):
        part = jnp.dot(
            zx[row : row + 32, lanes(b + start, stop - start)], kmat[b, start * OBS : stop * OBS, :],
            preferred_element_type=F32,
        )
        add(row // 2 + 16, b, 1, part[:, 0:128] + part[:, 128:256])

    def scatter(b, start, stop, row):
        vectors = zx[row : row + 32, lanes(b)]
        part = lax.dot_general(
            jnp.concatenate([vectors, vectors], axis=1), kmat[b, start * OBS : stop * OBS, :],
            (((1,), (1,)), ((), ())), preferred_element_type=F32,
        )
        add(row // 2 + 16, b + start, stop - start, part)

    last = NB

    def own_tiles(b, carry):
        for j in range(HALF):
            tile(b, j, own_mask(b, j))
        return carry

    def apply_own(b, row):
        gather(b, 0, HALF, row)
        scatter(b, 1, HALF, row)

    def first(b, carry):
        own_tiles(b, carry)
        apply_own(b, 0)
        return carry

    def second(b, carry):
        apply_own(b, 32)
        return carry

    def apply_last(row):
        for b in range(last, last + W):
            inside = last + W - b
            gather(b, 0, inside, row)
            if inside > 1:
                scatter(b, 1, inside, row)

    def apply_cross(row):
        for b in range(W):
            scatter(b, W - b, HALF, row)
            gather(last + b, W - b, HALF, row)

    lax.fori_loop(W, last, first, 0)
    for b in range(last, last + W):
        for j in range(last + W - b):
            tile(jnp.int32(b), j, own_mask(b, j))
    apply_last(0)
    for copy in static:
        copy.wait()

    def prepare_halo(i, carry):
        set_right(i, ens_lo[i], crd_lo[i])
        set_left(i + NB + W, ens_hi[i], crd_hi[i])
        set_vectors(i, v_lo[i])
        set_vectors(i + NB + W, v_hi[i])
        return carry

    lax.fori_loop(0, W, prepare_halo, 0)
    for b in range(W):
        for j in range(W - b, HALF):
            c = b + j
            tile(jnp.int32(b), j, maskx[W - j, c - W : c - W + 1, :])
            tile(jnp.int32(last + b), j, own_mask(last + b, j))
    apply_cross(0)

    moving = [
        remote(zf.at[16:32, (NB - W) * OBS : NB * OBS], p_lo, 6, right),
        remote(zf.at[16:32, 0 : W * OBS], p_hi, 7, left),
    ]
    for copy in moving:
        copy.start()

    def renew(row, source, start):
        hi, lo = split(source)
        zx[row : row + 16, start * OBS : start * OBS + source.shape[1]] = hi
        zx[row + 16 : row + 32, start * OBS : start * OBS + source.shape[1]] = lo

    product = zf[16:32, :]
    renew(32, product, W)

    def start_q(i, carry):
        zf[32:48, lanes(i)] = obs_v[pl.ds(i, 1), :] * zf[16:32, lanes(i)]
        return carry

    lax.fori_loop(0, NB, start_q, 0)
    lax.fori_loop(W, last, second, 0)
    apply_last(32)
    for copy in moving:
        copy.wait()
    renew(32, p_lo[...], 0)
    renew(32, p_hi[...], NB + W)
    apply_cross(32)
    renew(64, zf[32:48, :], W)

    inner = slice(W * OBS, (W + NB) * OBS)
    gram = lax.dot_general(
        zx[0:64, inner], zx[0:96, inner], (((1,), (1,)), ((), ())), preferred_element_type=F32
    )
    gram = jnp.concatenate([gram, jnp.zeros((64, 32), F32)], axis=1)
    lane = lax.broadcasted_iota(jnp.int32, (16, OBS), 1)
    lane8 = lax.broadcasted_iota(jnp.int32, (8, OBS), 1)

    def turn(value, by):
        return pltpu.roll(value, by % OBS, 1)

    of_r = gram[0:16] + gram[16:32]
    of_p = gram[32:48] + gram[48:64]
    of_r = of_r + turn(of_r, -16)
    of_p = of_p + turn(of_p, -16)
    even = (lane & 16) == 0
    own_part = jnp.where(even, of_r, turn(of_p, -16))
    part_a[...] = jnp.where(lane8 < 64, own_part[0:8], turn(own_part[8:16], 64))

    def exchange(part, red, peer, send, recv):
        def copy(step):
            return pltpu.make_async_remote_copy(
                src_ref=part, dst_ref=red.at[step - 1], send_sem=send.at[step - 1], recv_sem=recv.at[step - 1],
                device_id=peer(step), device_id_type=MESH,
            )

        def start(step, carry):
            copy(step).start()
            return carry

        def wait(step, carry):
            copy(step).wait()
            return carry

        lax.fori_loop(1, 16, start, 0)
        lax.fori_loop(1, 16, wait, 0)
        return part[...] + jnp.sum(red[...], axis=0)

    part_b[...] = exchange(part_a, red_a, peer_a, send_a, recv_a)
    packed = exchange(part_b, red_b, peer_b, send_b, recv_b)

    moments = jnp.concatenate([packed, turn(packed, 64)], axis=0)
    top = jnp.where(lane < 16, turn(moments, -32), jnp.where(lane < 32, moments, turn(moments, 32)))
    low = jnp.where(lane < 16, turn(moments, -16), jnp.where(lane < 32, turn(moments, -32), moments))
    system = jnp.concatenate([top, low], axis=0)
    rows = lax.broadcasted_iota(jnp.int32, (32, OBS), 0)
    for k in range(32):
        pivot = 1.0 / system[k : k + 1, k : k + 1]
        row = system[k : k + 1, :] * pivot
        system = jnp.where(rows == k, row, system - system[:, k : k + 1] * row)

    solved = jnp.concatenate([system, jnp.zeros((96, OBS), F32)], axis=0).T
    for_w = jnp.where(lane < 32, solved[32:48, :], 0.0)
    both = jnp.concatenate([for_w, turn(for_w, 16)], axis=0)[:, 0:48]
    for chunk in range(4):
        sums = jnp.dot(
            both, zf[:, chunk * 512 : (chunk + 1) * 512], preferred_element_type=F32, precision=lax.Precision.HIGHEST
        )
        for piece in range(4):
            b = chunk * 4 + piece
            here = sums[:, piece * OBS : (piece + 1) * OBS]
            out[b, 0:16, :] = here[0:16]
            out[b, 16:32, :] = zf[0:16, b * OBS : (b + 1) * OBS] - here[16:32]


def on_device(innovations, ensemble, coords, obs_error, pair_cols, pair_count):
    del pair_count
    out = pl.pallas_call(
        kernel,
        out_shape=jax.ShapeDtypeStruct((NB, 2 * RHS, OBS), F32),
        in_specs=[pl.BlockSpec(memory_space=pltpu.HBM)] * 5,
        out_specs=pl.BlockSpec(memory_space=pltpu.VMEM),
        scratch_shapes=[
            pltpu.VMEM((NB, MEM, OBS), F32),
            pltpu.VMEM((NB, 2, OBS), jnp.int32),
            pltpu.VMEM((NB, RHS, OBS), F32),
            pltpu.VMEM((NB, OBS), F32),
            pltpu.VMEM((NB, SLOTS), jnp.int32),
            pltpu.VMEM((NB + W, OBS, 256), BF16),
            pltpu.VMEM((NB + W, 256, 256), BF16),
            pltpu.VMEM((NB + W, HALF * OBS, 256), BF16),
            pltpu.VMEM((96, NX * OBS), BF16),
            pltpu.VMEM((48, NB * OBS), F32),
            pltpu.VMEM((SLOTS, NB, OBS), F32),
            pltpu.VMEM((W, MEM, OBS), F32),
            pltpu.VMEM((W, MEM, OBS), F32),
            pltpu.VMEM((W, 2, OBS), jnp.int32),
            pltpu.VMEM((W, 2, OBS), jnp.int32),
            pltpu.VMEM((W, RHS, OBS), F32),
            pltpu.VMEM((W, RHS, OBS), F32),
            pltpu.VMEM((RHS, W * OBS), F32),
            pltpu.VMEM((RHS, W * OBS), F32),
            pltpu.VMEM((8, OBS), F32),
            pltpu.VMEM((8, OBS), F32),
            pltpu.VMEM((15, 8, OBS), F32),
            pltpu.VMEM((15, 8, OBS), F32),
            pltpu.SemaphoreType.DMA((5,)),
            pltpu.SemaphoreType.DMA((8,)),
            pltpu.SemaphoreType.DMA((8,)),
            pltpu.SemaphoreType.DMA((15,)),
            pltpu.SemaphoreType.DMA((15,)),
            pltpu.SemaphoreType.DMA((15,)),
            pltpu.SemaphoreType.DMA((15,)),
        ],
        compiler_params=pltpu.CompilerParams(
            collective_id=0, has_side_effects=True, vmem_limit_bytes=56 * 1024 * 1024
        ),
    )(innovations, ensemble, coords, obs_error, pair_cols)
    return out[:, 0:RHS], out[:, RHS:]


def solution(mesh):
    both = ("region", "sub")
    in_specs = (
        P(both, None, None),
        P(both, None, None),
        P(both, None, None),
        P(both, None),
        P(both, None),
        P(both),
    )
    out_specs = (P(both, None, None), P(both, None, None))
    return jax.shard_map(on_device, mesh=mesh, in_specs=in_specs, out_specs=out_specs, check_vma=False)
```

```python
import jax
import jax.numpy as jnp
from jax import lax
from jax.experimental import pallas as pl
from jax.experimental.pallas import tpu as pltpu
from jax.sharding import PartitionSpec as P

MESH = pl.DeviceIdType.MESH
F32 = jnp.float32
BF16 = jnp.bfloat16

LIMIT = 40 * 1024 * 1024
NB = 16
W = 4
NX = NB + 2 * W
SLOTS = 2 * W + 1
HALF = W + 1
OBS = 128
RHS = 16
MEM = 64

STATIC_VAR = 0.002
LOG2E = 1.4426950408889634
C_CORR = -LOG2E / 150.0
C_LOC = -LOG2E / (2.0 * 200.0**2)
ENS_SCALE = 1.0 / ((MEM - 1) * STATIC_VAR)


def split(value):
    hi = value.astype(BF16)
    lo = (value - hi.astype(F32)).astype(BF16)
    return hi, lo


def half_first(value):
    first = value[:, 0:OBS] * 0.5
    return first if value.shape[1] == OBS else jnp.concatenate([first, value[:, OBS:]], axis=1)


def rows_of(rows):
    ids = lax.broadcasted_iota(jnp.int32, (16, OBS), 0)
    out = jnp.zeros((16, OBS), F32)
    for place, row in enumerate(rows):
        out = jnp.where(ids == place, jnp.broadcast_to(row, (16, OBS)), out)
    return out.astype(BF16)


def position_parts(crd, place):
    x = crd[0:1, :].astype(F32)
    y = crd[1:2, :].astype(F32)
    base = jnp.full((1, OBS), jnp.asarray(place - NX // 2).astype(F32) * 64.0, F32)
    full = x + base
    square = full * full + y * y
    s1 = square.astype(BF16).astype(F32)
    s2 = (square - s1).astype(BF16).astype(F32)
    s3 = square - s1 - s2
    return s1, s2, s3, base, x, y


def kernel(
    innov, ens, coords, obs, cols, zf, coeffs,
    ens_v, crd_v, v_v, obs_v, cols_v,
    lhsx, rhs, kmat, zx, maskx,
    ens_lo, ens_hi, crd_lo, crd_hi, v_lo, v_hi, p_lo, p_hi,
    part_a, part_b, red_a, red_b,
    load_sem, halo_send, halo_recv, send_a, recv_a, send_b, recv_b,
):
    me = lax.axis_index("region") * 4 + lax.axis_index("sub")

    def device(index):
        return (lax.div(index, 4), lax.rem(index, 4))

    left = device(lax.rem(me + 255, 256))
    right = device(lax.rem(me + 1, 256))
    x = lax.rem(me, 4)
    core = lax.rem(lax.div(me, 4), 2)
    y = lax.rem(lax.div(me, 8), 4)
    z = lax.div(me, 32)

    def peer_a(step):
        there = lax.rem(y * 4 + x + step, 16)
        return device(((z * 4 + lax.div(there, 4)) * 2 + core) * 4 + lax.rem(there, 4))

    def peer_b(step):
        there = lax.rem(z * 2 + core + step, 16)
        return device(((lax.div(there, 2) * 4 + y) * 2 + lax.rem(there, 2)) * 4 + x)

    barrier = pltpu.get_barrier_semaphore()
    for there in (left, right):
        pl.semaphore_signal(barrier, inc=1, device_id=there, device_id_type=MESH)

    def greet(step, carry):
        pl.semaphore_signal(barrier, inc=1, device_id=peer_a(step), device_id_type=MESH)
        pl.semaphore_signal(barrier, inc=1, device_id=peer_b(step), device_id_type=MESH)
        return carry

    lax.fori_loop(1, 16, greet, 0)
    loads = [
        pltpu.make_async_copy(source, target, load_sem.at[i])
        for i, (source, target) in enumerate(
            ((cols, cols_v), (coords, crd_v), (ens, ens_v), (innov, v_v), (obs, obs_v))
        )
    ]
    for load in loads:
        load.start()
    pl.semaphore_wait(barrier, 32)

    def remote(src, dst, slot, there):
        return pltpu.make_async_remote_copy(
            src_ref=src, dst_ref=dst, send_sem=halo_send.at[slot], recv_sem=halo_recv.at[slot],
            device_id=there, device_id_type=MESH,
        )

    small = [
        remote(coords.at[NB - W : NB], crd_lo, 0, right),
        remote(coords.at[0:W], crd_hi, 1, left),
        remote(innov.at[NB - W : NB], v_lo, 2, right),
        remote(innov.at[0:W], v_hi, 3, left),
    ]
    blocks = [
        (
            remote(ens.at[NB - 1 - q], ens_lo.at[W - 1 - q], 4 + 2 * q, right),
            remote(ens.at[q], ens_hi.at[q], 5 + 2 * q, left),
        )
        for q in range(W)
    ]
    for copy in small:
        copy.start()
    for pair in blocks:
        for copy in pair:
            copy.start()
    for load in loads:
        load.wait()

    offset = cols_v[...] - (lax.broadcasted_iota(jnp.int32, (NB, SLOTS), 0) + me * NB)
    for slot in range(SLOTS):
        hit = jnp.max(jnp.where(offset == slot - W, 1.0, 0.0).astype(F32), axis=1, keepdims=True)
        maskx[slot] = jnp.broadcast_to(hit, (NB, OBS))

    def lanes(place, count=1):
        return pl.ds(pl.multiple_of(place * OBS, OBS), count * OBS)

    def set_vectors(place, vectors):
        hi, lo = split(vectors)
        zx[0:16, lanes(place)] = hi
        zx[16:32, lanes(place)] = lo

    def set_left(place, members, crd):
        hi, lo = split(members)
        s1, s2, s3, base, x, y = position_parts(crd, place)
        one = jnp.ones((1, OBS), F32)
        parts = rows_of([s1, s2, s3, one, one, one, base, base, x, x, y])
        stacked = jnp.concatenate([hi, hi, lo, parts, jnp.zeros((48, OBS), BF16)], axis=0)
        lhsx[place - W] = stacked.T

    def set_right(place, members, crd):
        hi, lo = split(members * ENS_SCALE)
        s1, s2, s3, base, x, y = position_parts(crd, place)
        one = jnp.ones((1, OBS), F32)
        parts = rows_of([one, one, one, s1, s2, s3, -2.0 * base, -2.0 * x, -2.0 * base, -2.0 * x, -2.0 * y])
        rhs[place, 0:64, 0:128] = hi
        rhs[place, 64:128, 0:128] = lo
        rhs[place, 128:192, 0:128] = hi
        rhs[place, 192:256, 0:128] = jnp.zeros((64, OBS), BF16)
        rhs[place, 0:192, 128:256] = jnp.zeros((192, OBS), BF16)
        rhs[place, 192:208, 128:256] = parts
        rhs[place, 208:256, 128:256] = jnp.zeros((48, OBS), BF16)

    def prepare_own(i, carry):
        members = ens_v[i]
        vectors = v_v[i]
        set_left(i + W, members, crd_v[i])
        set_right(i + W, members, crd_v[i])
        set_vectors(i + W, vectors)
        zf[0:16, lanes(i)] = vectors
        zf[16:32, lanes(i)] = obs_v[pl.ds(i, 1), :] * vectors
        return carry

    lax.fori_loop(0, NB, prepare_own, 0)

    def tile(b, j, mask):
        both = jnp.dot(lhsx[b + j - W], rhs[b], preferred_element_type=F32)
        shared = both[:, 0:128]
        square = both[:, 128:256]
        inverse = lax.rsqrt(jnp.maximum(square, 1e-30))
        value = jnp.exp2(square * C_CORR * inverse) + jnp.exp2(square * C_LOC) * shared
        hi, lo = split(value * mask)
        kmat[b, j * OBS : (j + 1) * OBS, 0:128] = hi
        kmat[b, j * OBS : (j + 1) * OBS, 128:256] = lo

    def own_mask(b, j):
        return maskx[j + W, pl.ds(b - W, 1), :]

    def add(row, place, count, part):
        part = part[0:16] + part[16:32]
        zf[row : row + 16, lanes(place - W, count)] += part * STATIC_VAR

    def gather(b, start, stop, row):
        vectors = zx[row : row + 32, lanes(b + start, stop - start)]
        if row and start == 0:
            vectors = half_first(vectors)
        part = jnp.dot(
            vectors, kmat[b, start * OBS : stop * OBS, :],
            preferred_element_type=F32,
        )
        add(row // 2 + 16, b, 1, part[:, 0:128] + part[:, 128:256])

    def scatter(b, start, stop, row):
        vectors = zx[row : row + 32, lanes(b)]
        part = lax.dot_general(
            jnp.concatenate([vectors, vectors], axis=1), kmat[b, start * OBS : stop * OBS, :],
            (((1,), (1,)), ((), ())), preferred_element_type=F32,
        )
        if row and start == 0:
            part = half_first(part)
        add(row // 2 + 16, b + start, stop - start, part)

    last = NB

    def edge(b, carry):
        for j in range(HALF):
            tile(b, j, own_mask(b, j))
        gather(b, 0, HALF, 0)
        scatter(b, 1, HALF, 0)
        return carry

    lax.fori_loop(W, 2 * W, edge, 0)
    for b in range(last - W, last):
        for j in range(last - b, HALF):
            tile(b, j, own_mask(b, j))
        scatter(b, last - b, HALF, 0)
    for b in range(last, last + W):
        inside = last + W - b
        for j in range(inside):
            tile(b, j, own_mask(b, j))
        gather(b, 0, inside, 0)
        if inside > 1:
            scatter(b, 1, inside, 0)

    for copy in small:
        copy.wait()
    for q in range(W):
        set_vectors(q, v_lo[q])
        set_vectors(q + NB + W, v_hi[q])
    for q in range(W):
        for copy in blocks[q]:
            copy.wait()
        low, high = W - 1 - q, last + W + q
        set_right(low, ens_lo[low], crd_lo[low])
        set_left(high, ens_hi[q], crd_hi[q])
        for j in range(q + 1, HALF):
            c = low + j
            tile(low, j, maskx[W - j, c - W : c - W + 1, :])
            tile(high - j, j, own_mask(high - j, j))
        scatter(low, q + 1, HALF, 0)
        for j in range(q + 1, HALF):
            gather(high - j, j, j + 1, 0)

    moving = [
        remote(zf.at[16:32, 0 : W * OBS], p_hi, 12, left),
        remote(zf.at[16:32, (NB - W) * OBS : NB * OBS], p_lo, 13, right),
    ]
    for copy in moving:
        copy.start()

    def inner(b, carry):
        for j in range(HALF):
            tile(b, j, own_mask(b, j))
        gather(b, 0, HALF, 0)
        scatter(b, 1, HALF, 0)
        return carry

    lax.fori_loop(2 * W, last - W, inner, 0)
    for b in range(last - W, last):
        for j in range(last - b):
            tile(b, j, own_mask(b, j))
        gather(b, 0, HALF, 0)
        if last - b > 1:
            scatter(b, 1, last - b, 0)

    def renew(row, source, start):
        hi, lo = split(source)
        zx[row : row + 16, start * OBS : start * OBS + source.shape[1]] = hi
        zx[row + 16 : row + 32, start * OBS : start * OBS + source.shape[1]] = lo

    renew(32, zf[16:32, :], W)

    def upper(b, carry):
        zf[32:48, lanes(b - W)] = 0.5 * obs_v[pl.ds(b - W, 1), :] * zf[16:32, lanes(b - W)]
        gather(b, 0, HALF, 32)
        return carry

    lax.fori_loop(W, last, upper, 0)
    for b in range(last, last + W):
        upper_lanes = lanes(b - W)
        zf[32:48, upper_lanes] = 0.5 * obs_v[b - W : b - W + 1, :] * zf[16:32, upper_lanes]
        gather(b, 0, last + W - b, 32)
    for copy in moving:
        copy.wait()
    renew(32, p_hi[...], NB + W)
    for b in range(last, last + W):
        gather(b, last + W - b, HALF, 32)
    renew(64, zf[32:48, :], W)

    inner = slice(W * OBS, (W + NB) * OBS)
    gram = lax.dot_general(
        zx[0:64, inner], zx[0:96, inner], (((1,), (1,)), ((), ())), preferred_element_type=F32
    )
    gram = jnp.concatenate([gram, jnp.zeros((64, 32), F32)], axis=1)
    lane = lax.broadcasted_iota(jnp.int32, (16, OBS), 1)
    lane8 = lax.broadcasted_iota(jnp.int32, (8, OBS), 1)

    def turn(value, by):
        return pltpu.roll(value, by % OBS, 1)

    of_r = gram[0:16] + gram[16:32]
    of_p = gram[32:48] + gram[48:64]
    of_r = of_r + turn(of_r, -16)
    of_p = of_p + turn(of_p, -16)
    even = (lane & 16) == 0
    own_part = jnp.where(even, of_r, turn(of_p, -16))
    part_a[...] = jnp.where(lane8 < 64, own_part[0:8], turn(own_part[8:16], 64))

    def exchange(part, red, peer, send, recv):
        copies = [
            pltpu.make_async_remote_copy(
                src_ref=part, dst_ref=red.at[step - 1], send_sem=send.at[step - 1], recv_sem=recv.at[step - 1],
                device_id=peer(step), device_id_type=MESH,
            )
            for step in range(1, 16)
        ]
        for copy in copies:
            copy.start()
        return copies

    first_sum = exchange(part_a, red_a, peer_a, send_a, recv_a)

    def rest(b, carry):
        scatter(b, 0, HALF, 32)
        return carry

    renew(32, p_lo[...], 0)
    for b in range(W):
        scatter(b, W - b, HALF, 32)
    lax.fori_loop(W, last, rest, 0)
    for b in range(last, last + W):
        scatter(b, 0, last + W - b, 32)

    def other_half(i, carry):
        zf[32:48, lanes(i)] += 0.5 * obs_v[pl.ds(i, 1), :] * zf[16:32, lanes(i)]
        return carry

    lax.fori_loop(0, NB, other_half, 0)
    for copy in first_sum:
        copy.wait()
    part_b[...] = part_a[...] + jnp.sum(red_a[...], axis=0)
    second_sum = exchange(part_b, red_b, peer_b, send_b, recv_b)
    for copy in second_sum:
        copy.wait()
    packed = part_b[...] + jnp.sum(red_b[...], axis=0)

    moments = jnp.concatenate([packed, turn(packed, 64)], axis=0)
    top = jnp.where(lane < 16, turn(moments, -32), jnp.where(lane < 32, moments, turn(moments, 32)))
    low = jnp.where(lane < 16, turn(moments, -16), jnp.where(lane < 32, turn(moments, -32), moments))
    system = jnp.concatenate([top, low], axis=0)
    rows = lax.broadcasted_iota(jnp.int32, (32, OBS), 0)
    half = jnp.where((lane >= 16) & (lane < 32), system[16:32], 0.0)
    flipped = jnp.concatenate([half, jnp.zeros((112, OBS), F32)], axis=0).T[16:32, :]
    system = jnp.concatenate([system[0:16], system[16:32] + turn(flipped, 16)], axis=0)
    for k in range(0, 32, 2):
        row0, row1 = system[k : k + 1, :], system[k + 1 : k + 2, :]
        a, b = row0[:, k : k + 1], row0[:, k + 1 : k + 2]
        c, d = row1[:, k : k + 1], row1[:, k + 1 : k + 2]
        scale = 1.0 / (a * d - b * c)
        new0 = (d * row0 - b * row1) * scale
        new1 = (a * row1 - c * row0) * scale
        rest_of = system - system[:, k : k + 1] * new0 - system[:, k + 1 : k + 2] * new1
        system = jnp.where(rows == k, new0, jnp.where(rows == k + 1, new1, rest_of))

    solved = jnp.concatenate([system, jnp.zeros((96, OBS), F32)], axis=0).T
    for_w = jnp.where(lane < 32, solved[32:48, :], 0.0)
    coeffs[...] = jnp.concatenate([for_w, turn(for_w, 16)], axis=0)


def combine(coeffs, zf, w_out, r_out):
    count = w_out.shape[0]
    here = pl.ds(pl.multiple_of(pl.program_id(0) * count * OBS, OBS), count * OBS)
    sums = jnp.dot(
        coeffs[:, 0:48], zf[:, here], preferred_element_type=F32, precision=lax.Precision.HIGHEST
    )
    rest = zf[0:16, here] - sums[16:32]
    for b in range(count):
        w_out[b] = sums[0:16, b * OBS : (b + 1) * OBS]
        r_out[b] = rest[:, b * OBS : (b + 1) * OBS]


def on_device(innovations, ensemble, coords, obs_error, pair_cols, pair_count):
    del pair_count
    vmem = pl.BlockSpec(memory_space=pltpu.VMEM)
    arrays = [pltpu.with_memory_space_constraint(a, pltpu.HBM) for a in (innovations, ensemble, coords, obs_error, pair_cols)]
    vectors, coeffs = pl.pallas_call(
        kernel,
        out_shape=(jax.ShapeDtypeStruct((48, NB * OBS), F32), jax.ShapeDtypeStruct((32, OBS), F32)),
        in_specs=[pl.BlockSpec(memory_space=pltpu.HBM)] * 5,
        out_specs=(vmem, vmem),
        scratch_shapes=[
            pltpu.VMEM((NB, MEM, OBS), F32),
            pltpu.VMEM((NB, 2, OBS), jnp.int32),
            pltpu.VMEM((NB, RHS, OBS), F32),
            pltpu.VMEM((NB, OBS), F32),
            pltpu.VMEM((NB, SLOTS), jnp.int32),
            pltpu.VMEM((NB + W, OBS, 256), BF16),
            pltpu.VMEM((NB + W, 256, 256), BF16),
            pltpu.VMEM((NB + W, HALF * OBS, 256), BF16),
            pltpu.VMEM((96, NX * OBS), BF16),
            pltpu.VMEM((SLOTS, NB, OBS), F32),
            pltpu.VMEM((W, MEM, OBS), F32),
            pltpu.VMEM((W, MEM, OBS), F32),
            pltpu.VMEM((W, 2, OBS), jnp.int32),
            pltpu.VMEM((W, 2, OBS), jnp.int32),
            pltpu.VMEM((W, RHS, OBS), F32),
            pltpu.VMEM((W, RHS, OBS), F32),
            pltpu.VMEM((RHS, W * OBS), F32),
            pltpu.VMEM((RHS, W * OBS), F32),
            pltpu.VMEM((8, OBS), F32),
            pltpu.VMEM((8, OBS), F32),
            pltpu.VMEM((15, 8, OBS), F32),
            pltpu.VMEM((15, 8, OBS), F32),
            pltpu.SemaphoreType.DMA((5,)),
            pltpu.SemaphoreType.DMA((14,)),
            pltpu.SemaphoreType.DMA((14,)),
            pltpu.SemaphoreType.DMA((15,)),
            pltpu.SemaphoreType.DMA((15,)),
            pltpu.SemaphoreType.DMA((15,)),
            pltpu.SemaphoreType.DMA((15,)),
        ],
        compiler_params=pltpu.CompilerParams(
            collective_id=0, has_side_effects=True, vmem_limit_bytes=LIMIT
        ),
    )(*arrays)
    count = 4
    out = jax.ShapeDtypeStruct((NB, RHS, OBS), F32)
    piece = pl.BlockSpec((count, RHS, OBS), lambda i: (i, 0, 0))
    return pl.pallas_call(
        combine, out_shape=(out, out), grid=(NB // count,), in_specs=[vmem, vmem], out_specs=(piece, piece)
    )(coeffs, vectors)


def solution(mesh):
    both = ("region", "sub")
    in_specs = (
        P(both, None, None),
        P(both, None, None),
        P(both, None, None),
        P(both, None),
        P(both, None),
        P(both),
    )
    out_specs = (P(both, None, None), P(both, None, None))
    return jax.shard_map(on_device, mesh=mesh, in_specs=in_specs, out_specs=out_specs, check_vma=False)
```

```python
import jax
import jax.numpy as jnp
from jax import lax
from jax.experimental import pallas as pl
from jax.experimental.pallas import tpu as pltpu
from jax.sharding import PartitionSpec as P

MESH = pl.DeviceIdType.MESH
F32 = jnp.float32
BF16 = jnp.bfloat16

LIMIT = 40 * 1024 * 1024
EARLY = 2
NB = 16
W = 4
NX = NB + 2 * W
SLOTS = 2 * W + 1
HALF = W + 1
OBS = 128
RHS = 16
MEM = 64

STATIC_VAR = 0.002
LOG2E = 1.4426950408889634
C_CORR = -LOG2E / 150.0
C_LOC = -LOG2E / (2.0 * 200.0**2)
ENS_SCALE = 1.0 / ((MEM - 1) * STATIC_VAR)


def split(value):
    hi = value.astype(BF16)
    lo = (value - hi.astype(F32)).astype(BF16)
    return hi, lo


def half_first(value):
    first = value[:, 0:OBS] * 0.5
    return first if value.shape[1] == OBS else jnp.concatenate([first, value[:, OBS:]], axis=1)


def rows_of(rows):
    ids = lax.broadcasted_iota(jnp.int32, (16, OBS), 0)
    out = jnp.zeros((16, OBS), F32)
    for place, row in enumerate(rows):
        out = jnp.where(ids == place, jnp.broadcast_to(row, (16, OBS)), out)
    return out.astype(BF16)


def position_parts(crd, place):
    x = crd[0:1, :].astype(F32)
    y = crd[1:2, :].astype(F32)
    base = jnp.full((1, OBS), jnp.asarray(place - NX // 2).astype(F32) * 64.0, F32)
    full = x + base
    square = full * full + y * y
    s1 = square.astype(BF16).astype(F32)
    s2 = (square - s1).astype(BF16).astype(F32)
    s3 = square - s1 - s2
    return s1, s2, s3, base, x, y


def kernel(
    innov, ens, coords, obs, cols, w_out, r_out,
    ens_v, crd_v, v_v, obs_v, cols_v,
    lhsx, rhs, kmat, zx, zf, maskx,
    ens_lo, ens_hi, crd_lo, crd_hi, v_lo, v_hi, p_lo, p_hi,
    part_a, part_b, red_a, red_b,
    load_sem, halo_send, halo_recv, send_a, recv_a, send_b, recv_b,
):
    me = lax.axis_index("region") * 4 + lax.axis_index("sub")

    def device(index):
        return (lax.div(index, 4), lax.rem(index, 4))

    left = device(lax.rem(me + 255, 256))
    right = device(lax.rem(me + 1, 256))
    x = lax.rem(me, 4)
    core = lax.rem(lax.div(me, 4), 2)
    y = lax.rem(lax.div(me, 8), 4)
    z = lax.div(me, 32)

    def peer_a(step):
        there = lax.rem(y * 4 + x + step, 16)
        return device(((z * 4 + lax.div(there, 4)) * 2 + core) * 4 + lax.rem(there, 4))

    def peer_b(step):
        there = lax.rem(z * 2 + core + step, 16)
        return device(((lax.div(there, 2) * 4 + y) * 2 + lax.rem(there, 2)) * 4 + x)

    barrier = pltpu.get_barrier_semaphore()
    for there in (left, right):
        pl.semaphore_signal(barrier, inc=1, device_id=there, device_id_type=MESH)

    def greet(step, carry):
        pl.semaphore_signal(barrier, inc=1, device_id=peer_a(step), device_id_type=MESH)
        pl.semaphore_signal(barrier, inc=1, device_id=peer_b(step), device_id_type=MESH)
        return carry

    lax.fori_loop(1, 16, greet, 0)
    loads = [
        pltpu.make_async_copy(source, target, load_sem.at[i])
        for i, (source, target) in enumerate(
            ((cols, cols_v), (coords, crd_v), (ens, ens_v), (innov, v_v), (obs, obs_v))
        )
    ]
    for load in loads:
        load.start()
    pl.semaphore_wait(barrier, 32)

    def remote(src, dst, slot, there):
        return pltpu.make_async_remote_copy(
            src_ref=src, dst_ref=dst, send_sem=halo_send.at[slot], recv_sem=halo_recv.at[slot],
            device_id=there, device_id_type=MESH,
        )

    small = [
        remote(coords.at[NB - W : NB], crd_lo, 0, right),
        remote(coords.at[0:W], crd_hi, 1, left),
        remote(innov.at[NB - W : NB], v_lo, 2, right),
        remote(innov.at[0:W], v_hi, 3, left),
    ]
    blocks = [
        (
            remote(ens.at[NB - 1 - q], ens_lo.at[W - 1 - q], 4 + 2 * q, right),
            remote(ens.at[q], ens_hi.at[q], 5 + 2 * q, left),
        )
        for q in range(W)
    ]
    for copy in small:
        copy.start()
    for pair in blocks:
        for copy in pair:
            copy.start()
    for load in loads:
        load.wait()

    offset = cols_v[...] - (lax.broadcasted_iota(jnp.int32, (NB, SLOTS), 0) + me * NB)
    for slot in range(SLOTS):
        hit = jnp.max(jnp.where(offset == slot - W, 1.0, 0.0).astype(F32), axis=1, keepdims=True)
        maskx[slot] = jnp.broadcast_to(hit, (NB, OBS))

    def lanes(place, count=1):
        return pl.ds(pl.multiple_of(place * OBS, OBS), count * OBS)

    def set_vectors(place, vectors):
        hi, lo = split(vectors)
        zx[0:16, lanes(place)] = hi
        zx[16:32, lanes(place)] = lo

    def set_left(place, members, crd):
        hi, lo = split(members)
        s1, s2, s3, base, x, y = position_parts(crd, place)
        one = jnp.ones((1, OBS), F32)
        parts = rows_of([s1, s2, s3, one, one, one, base, base, x, x, y])
        stacked = jnp.concatenate([hi, hi, lo, parts, jnp.zeros((48, OBS), BF16)], axis=0)
        lhsx[place - W] = stacked.T

    def set_right(place, members, crd):
        hi, lo = split(members * ENS_SCALE)
        s1, s2, s3, base, x, y = position_parts(crd, place)
        one = jnp.ones((1, OBS), F32)
        parts = rows_of([one, one, one, s1, s2, s3, -2.0 * base, -2.0 * x, -2.0 * base, -2.0 * x, -2.0 * y])
        rhs[place, 0:64, 0:128] = hi
        rhs[place, 64:128, 0:128] = lo
        rhs[place, 128:192, 0:128] = hi
        rhs[place, 192:256, 0:128] = jnp.zeros((64, OBS), BF16)
        rhs[place, 0:192, 128:256] = jnp.zeros((192, OBS), BF16)
        rhs[place, 192:208, 128:256] = parts
        rhs[place, 208:256, 128:256] = jnp.zeros((48, OBS), BF16)

    def prepare_own(i, carry):
        members = ens_v[i]
        vectors = v_v[i]
        set_left(i + W, members, crd_v[i])
        set_right(i + W, members, crd_v[i])
        set_vectors(i + W, vectors)
        zf[0:16, lanes(i)] = vectors
        zf[16:32, lanes(i)] = obs_v[pl.ds(i, 1), :] * vectors
        return carry

    lax.fori_loop(0, NB, prepare_own, 0)

    def tile(b, j, mask):
        both = jnp.dot(lhsx[b + j - W], rhs[b], preferred_element_type=F32)
        shared = both[:, 0:128]
        square = both[:, 128:256]
        inverse = lax.rsqrt(jnp.maximum(square, 1e-30))
        value = jnp.exp2(square * C_CORR * inverse) + jnp.exp2(square * C_LOC) * shared
        hi, lo = split(value * mask)
        kmat[b, j * OBS : (j + 1) * OBS, 0:128] = hi
        kmat[b, j * OBS : (j + 1) * OBS, 128:256] = lo

    def own_mask(b, j):
        return maskx[j + W, pl.ds(b - W, 1), :]

    def add(row, place, count, part):
        part = part[0:16] + part[16:32]
        zf[row : row + 16, lanes(place - W, count)] += part * STATIC_VAR

    def gather(b, start, stop, row):
        vectors = zx[row : row + 32, lanes(b + start, stop - start)]
        if row and start == 0:
            vectors = half_first(vectors)
        part = jnp.dot(
            vectors, kmat[b, start * OBS : stop * OBS, :],
            preferred_element_type=F32,
        )
        add(row // 2 + 16, b, 1, part[:, 0:128] + part[:, 128:256])

    def scatter(b, start, stop, row):
        vectors = zx[row : row + 32, lanes(b)]
        part = lax.dot_general(
            jnp.concatenate([vectors, vectors], axis=1), kmat[b, start * OBS : stop * OBS, :],
            (((1,), (1,)), ((), ())), preferred_element_type=F32,
        )
        if row and start == 0:
            part = half_first(part)
        add(row // 2 + 16, b + start, stop - start, part)

    last = NB

    def edge(b, carry):
        for j in range(HALF):
            tile(b, j, own_mask(b, j))
        gather(b, 0, HALF, 0)
        scatter(b, 1, HALF, 0)
        return carry

    lax.fori_loop(W, 2 * W + EARLY, edge, 0)
    for b in range(last - W, last):
        for j in range(last - b, HALF):
            tile(b, j, own_mask(b, j))
        scatter(b, last - b, HALF, 0)
    for b in range(last, last + W):
        inside = last + W - b
        for j in range(inside):
            tile(b, j, own_mask(b, j))
        gather(b, 0, inside, 0)
        if inside > 1:
            scatter(b, 1, inside, 0)

    for copy in small:
        copy.wait()
    for q in range(W):
        set_vectors(q, v_lo[q])
        set_vectors(q + NB + W, v_hi[q])
    for q in range(W):
        for copy in blocks[q]:
            copy.wait()
        low, high = W - 1 - q, last + W + q
        set_right(low, ens_lo[low], crd_lo[low])
        set_left(high, ens_hi[q], crd_hi[q])
        for j in range(q + 1, HALF):
            c = low + j
            tile(low, j, maskx[W - j, c - W : c - W + 1, :])
            tile(high - j, j, own_mask(high - j, j))
        scatter(low, q + 1, HALF, 0)
        for j in range(q + 1, HALF):
            gather(high - j, j, j + 1, 0)

    moving = [
        remote(zf.at[16:32, 0 : W * OBS], p_hi, 12, left),
        remote(zf.at[16:32, (NB - W) * OBS : NB * OBS], p_lo, 13, right),
    ]
    for copy in moving:
        copy.start()

    lax.fori_loop(2 * W + EARLY, last - W, edge, 0)
    for b in range(last - W, last):
        for j in range(last - b):
            tile(b, j, own_mask(b, j))
        gather(b, 0, HALF, 0)
        if last - b > 1:
            scatter(b, 1, last - b, 0)

    def renew(row, source, start):
        hi, lo = split(source)
        zx[row : row + 16, start * OBS : start * OBS + source.shape[1]] = hi
        zx[row + 16 : row + 32, start * OBS : start * OBS + source.shape[1]] = lo

    renew(32, zf[16:32, :], W)

    def upper(b, carry):
        zf[32:48, lanes(b - W)] = 0.5 * obs_v[pl.ds(b - W, 1), :] * zf[16:32, lanes(b - W)]
        gather(b, 0, HALF, 32)
        return carry

    lax.fori_loop(W, last, upper, 0)
    for b in range(last, last + W):
        upper_lanes = lanes(b - W)
        zf[32:48, upper_lanes] = 0.5 * obs_v[b - W : b - W + 1, :] * zf[16:32, upper_lanes]
        gather(b, 0, last + W - b, 32)
    for copy in moving:
        copy.wait()
    renew(32, p_hi[...], NB + W)
    for b in range(last, last + W):
        gather(b, last + W - b, HALF, 32)
    renew(64, zf[32:48, :], W)

    inner = slice(W * OBS, (W + NB) * OBS)
    gram = lax.dot_general(
        zx[0:64, inner], zx[0:96, inner], (((1,), (1,)), ((), ())), preferred_element_type=F32
    )
    gram = jnp.concatenate([gram, jnp.zeros((64, 32), F32)], axis=1)
    lane = lax.broadcasted_iota(jnp.int32, (16, OBS), 1)
    lane8 = lax.broadcasted_iota(jnp.int32, (8, OBS), 1)

    def turn(value, by):
        return pltpu.roll(value, by % OBS, 1)

    of_r = gram[0:16] + gram[16:32]
    of_p = gram[32:48] + gram[48:64]
    of_r = of_r + turn(of_r, -16)
    of_p = of_p + turn(of_p, -16)
    even = (lane & 16) == 0
    own_part = jnp.where(even, of_r, turn(of_p, -16))
    part_a[...] = jnp.where(lane8 < 64, own_part[0:8], turn(own_part[8:16], 64))

    def exchange(part, red, peer, send, recv):
        copies = [
            pltpu.make_async_remote_copy(
                src_ref=part, dst_ref=red.at[step - 1], send_sem=send.at[step - 1], recv_sem=recv.at[step - 1],
                device_id=peer(step), device_id_type=MESH,
            )
            for step in range(1, 16)
        ]
        for copy in copies:
            copy.start()
        return copies

    first_sum = exchange(part_a, red_a, peer_a, send_a, recv_a)

    def rest(b, carry):
        scatter(b, 0, HALF, 32)
        return carry

    renew(32, p_lo[...], 0)
    for b in range(W):
        scatter(b, W - b, HALF, 32)
    lax.fori_loop(W, last, rest, 0)
    for b in range(last, last + W):
        scatter(b, 0, last + W - b, 32)

    def other_half(i, carry):
        zf[32:48, lanes(i)] += 0.5 * obs_v[pl.ds(i, 1), :] * zf[16:32, lanes(i)]
        return carry

    lax.fori_loop(0, NB, other_half, 0)
    for copy in first_sum:
        copy.wait()
    part_b[...] = part_a[...] + jnp.sum(red_a[...], axis=0)
    second_sum = exchange(part_b, red_b, peer_b, send_b, recv_b)
    for copy in second_sum:
        copy.wait()
    packed = part_b[...] + jnp.sum(red_b[...], axis=0)

    moments = jnp.concatenate([packed, turn(packed, 64)], axis=0)
    top = jnp.where(lane < 16, turn(moments, -32), jnp.where(lane < 32, moments, turn(moments, 32)))
    low = jnp.where(lane < 16, turn(moments, -16), jnp.where(lane < 32, turn(moments, -32), moments))
    system = jnp.concatenate([top, low], axis=0)
    rows = lax.broadcasted_iota(jnp.int32, (32, OBS), 0)
    half = jnp.where((lane >= 16) & (lane < 32), system[16:32], 0.0)
    flipped = jnp.concatenate([half, jnp.zeros((112, OBS), F32)], axis=0).T[16:32, :]
    system = jnp.concatenate([system[0:16], system[16:32] + turn(flipped, 16)], axis=0)
    spread = [jnp.broadcast_to(system[:, j : j + 1], (32, OBS)) for j in range(32)]
    inverses = []
    for k in range(32):
        inverse = 1.0 / spread[k][k : k + 1, :]
        factor = jnp.where(rows == k, 0.0, spread[k] * inverse)
        for j in range(k + 1, 32):
            spread[j] = spread[j] - factor * spread[j][k : k + 1, :]
        system = system - factor * system[k : k + 1, :]
        inverses.append(inverse)
    system = system * jnp.concatenate(inverses, axis=0)

    solved = jnp.concatenate([system, jnp.zeros((96, OBS), F32)], axis=0).T
    for_w = jnp.where(lane < 32, solved[32:48, :], 0.0)
    both = jnp.concatenate([for_w, turn(for_w, 16)], axis=0)[:, 0:48]
    for chunk in range(4):
        here = slice(chunk * 4 * OBS, (chunk + 1) * 4 * OBS)
        sums = jnp.dot(both, zf[:, here], preferred_element_type=F32, precision=lax.Precision.HIGHEST)
        left_over = zf[0:16, here] - sums[16:32]
        for piece in range(4):
            b = chunk * 4 + piece
            w_out[b] = sums[0:16, piece * OBS : (piece + 1) * OBS]
            r_out[b] = left_over[:, piece * OBS : (piece + 1) * OBS]


def on_device(innovations, ensemble, coords, obs_error, pair_cols, pair_count):
    del pair_count
    vmem = pl.BlockSpec(memory_space=pltpu.VMEM)
    arrays = [pltpu.with_memory_space_constraint(a, pltpu.HBM) for a in (innovations, ensemble, coords, obs_error, pair_cols)]
    out = jax.ShapeDtypeStruct((NB, RHS, OBS), F32)
    return pl.pallas_call(
        kernel,
        out_shape=(out, out),
        in_specs=[pl.BlockSpec(memory_space=pltpu.HBM)] * 5,
        out_specs=(vmem, vmem),
        scratch_shapes=[
            pltpu.VMEM((NB, MEM, OBS), F32),
            pltpu.VMEM((NB, 2, OBS), jnp.int32),
            pltpu.VMEM((NB, RHS, OBS), F32),
            pltpu.VMEM((NB, OBS), F32),
            pltpu.VMEM((NB, SLOTS), jnp.int32),
            pltpu.VMEM((NB + W, OBS, 256), BF16),
            pltpu.VMEM((NB + W, 256, 256), BF16),
            pltpu.VMEM((NB + W, HALF * OBS, 256), BF16),
            pltpu.VMEM((96, NX * OBS), BF16),
            pltpu.VMEM((48, NB * OBS), F32),
            pltpu.VMEM((SLOTS, NB, OBS), F32),
            pltpu.VMEM((W, MEM, OBS), F32),
            pltpu.VMEM((W, MEM, OBS), F32),
            pltpu.VMEM((W, 2, OBS), jnp.int32),
            pltpu.VMEM((W, 2, OBS), jnp.int32),
            pltpu.VMEM((W, RHS, OBS), F32),
            pltpu.VMEM((W, RHS, OBS), F32),
            pltpu.VMEM((RHS, W * OBS), F32),
            pltpu.VMEM((RHS, W * OBS), F32),
            pltpu.VMEM((8, OBS), F32),
            pltpu.VMEM((8, OBS), F32),
            pltpu.VMEM((15, 8, OBS), F32),
            pltpu.VMEM((15, 8, OBS), F32),
            pltpu.SemaphoreType.DMA((5,)),
            pltpu.SemaphoreType.DMA((14,)),
            pltpu.SemaphoreType.DMA((14,)),
            pltpu.SemaphoreType.DMA((15,)),
            pltpu.SemaphoreType.DMA((15,)),
            pltpu.SemaphoreType.DMA((15,)),
            pltpu.SemaphoreType.DMA((15,)),
        ],
        compiler_params=pltpu.CompilerParams(
            collective_id=0, has_side_effects=True, vmem_limit_bytes=LIMIT
        ),
    )(*arrays)


def solution(mesh):
    both = ("region", "sub")
    in_specs = (
        P(both, None, None),
        P(both, None, None),
        P(both, None, None),
        P(both, None),
        P(both, None),
        P(both),
    )
    out_specs = (P(both, None, None), P(both, None, None))
    return jax.shard_map(on_device, mesh=mesh, in_specs=in_specs, out_specs=out_specs, check_vma=False)
```

```python
import jax
import jax.numpy as jnp
from jax import lax
from jax.experimental import pallas as pl
from jax.experimental.pallas import tpu as pltpu
from jax.sharding import PartitionSpec as P

MESH = pl.DeviceIdType.MESH
F32 = jnp.float32
BF16 = jnp.bfloat16

LIMIT = 40 * 1024 * 1024
UNROLL = 4
EARLY = 3
NB = 16
W = 4
NX = NB + 2 * W
SLOTS = 2 * W + 1
HALF = W + 1
OBS = 128
RHS = 16
MEM = 64

STATIC_VAR = 0.002
LOG2E = 1.4426950408889634
C_CORR = -LOG2E / 150.0
C_LOC = -LOG2E / (2.0 * 200.0**2)
ENS_SCALE = 1.0 / ((MEM - 1) * STATIC_VAR)


def split(value):
    hi = value.astype(BF16)
    lo = (value - hi.astype(F32)).astype(BF16)
    return hi, lo


def half_first(value):
    first = value[:, 0:OBS] * 0.5
    return first if value.shape[1] == OBS else jnp.concatenate([first, value[:, OBS:]], axis=1)


def rows_of(rows):
    ids = lax.broadcasted_iota(jnp.int32, (16, OBS), 0)
    out = jnp.zeros((16, OBS), F32)
    for place, row in enumerate(rows):
        out = jnp.where(ids == place, jnp.broadcast_to(row, (16, OBS)), out)
    return out.astype(BF16)


def position_parts(crd, place):
    x = crd[0:1, :].astype(F32)
    y = crd[1:2, :].astype(F32)
    base = jnp.full((1, OBS), jnp.asarray(place - NX // 2).astype(F32) * 64.0, F32)
    full = x + base
    square = full * full + y * y
    s1 = square.astype(BF16).astype(F32)
    s2 = (square - s1).astype(BF16).astype(F32)
    s3 = square - s1 - s2
    return s1, s2, s3, base, x, y


def kernel(
    innov, ens, coords, obs, cols, w_out, r_out,
    ens_v, crd_v, v_v, obs_v, cols_v,
    lhsx, rhs, kmat, zx, zf, maskx,
    ens_lo, ens_hi, crd_lo, crd_hi, v_lo, v_hi, p_lo, p_hi,
    part_a, part_b, red_a, red_b,
    load_sem, halo_send, halo_recv, send_a, recv_a, send_b, recv_b,
):
    me = lax.axis_index("region") * 4 + lax.axis_index("sub")

    def device(index):
        return (lax.div(index, 4), lax.rem(index, 4))

    left = device(lax.rem(me + 255, 256))
    right = device(lax.rem(me + 1, 256))
    x = lax.rem(me, 4)
    core = lax.rem(lax.div(me, 4), 2)
    y = lax.rem(lax.div(me, 8), 4)
    z = lax.div(me, 32)

    def peer_a(step):
        there = lax.rem(y * 4 + x + step, 16)
        return device(((z * 4 + lax.div(there, 4)) * 2 + core) * 4 + lax.rem(there, 4))

    def peer_b(step):
        there = lax.rem(z * 2 + core + step, 16)
        return device(((lax.div(there, 2) * 4 + y) * 2 + lax.rem(there, 2)) * 4 + x)

    barrier = pltpu.get_barrier_semaphore()
    for there in (left, right):
        pl.semaphore_signal(barrier, inc=1, device_id=there, device_id_type=MESH)

    def greet(step, carry):
        pl.semaphore_signal(barrier, inc=1, device_id=peer_a(step), device_id_type=MESH)
        pl.semaphore_signal(barrier, inc=1, device_id=peer_b(step), device_id_type=MESH)
        return carry

    lax.fori_loop(1, 16, greet, 0)
    loads = [
        pltpu.make_async_copy(source, target, load_sem.at[i])
        for i, (source, target) in enumerate(
            ((cols, cols_v), (coords, crd_v), (ens, ens_v), (innov, v_v), (obs, obs_v))
        )
    ]
    for load in loads:
        load.start()
    pl.semaphore_wait(barrier, 32)

    def remote(src, dst, slot, there):
        return pltpu.make_async_remote_copy(
            src_ref=src, dst_ref=dst, send_sem=halo_send.at[slot], recv_sem=halo_recv.at[slot],
            device_id=there, device_id_type=MESH,
        )

    small = [
        remote(coords.at[NB - W : NB], crd_lo, 0, right),
        remote(coords.at[0:W], crd_hi, 1, left),
        remote(innov.at[NB - W : NB], v_lo, 2, right),
        remote(innov.at[0:W], v_hi, 3, left),
    ]
    blocks = [
        (
            remote(ens.at[NB - 1 - q], ens_lo.at[W - 1 - q], 4 + 2 * q, right),
            remote(ens.at[q], ens_hi.at[q], 5 + 2 * q, left),
        )
        for q in range(W)
    ]
    for copy in small:
        copy.start()
    for pair in blocks:
        for copy in pair:
            copy.start()
    for load in loads:
        load.wait()

    offset = cols_v[...] - (lax.broadcasted_iota(jnp.int32, (NB, SLOTS), 0) + me * NB)
    for slot in range(SLOTS):
        hit = jnp.max(jnp.where(offset == slot - W, 1.0, 0.0).astype(F32), axis=1, keepdims=True)
        maskx[slot] = jnp.broadcast_to(hit, (NB, OBS))

    def lanes(place, count=1):
        return pl.ds(pl.multiple_of(place * OBS, OBS), count * OBS)

    def set_vectors(place, vectors):
        hi, lo = split(vectors)
        zx[0:16, lanes(place)] = hi
        zx[16:32, lanes(place)] = lo

    def set_left(place, members, crd):
        hi, lo = split(members)
        s1, s2, s3, base, x, y = position_parts(crd, place)
        one = jnp.ones((1, OBS), F32)
        parts = rows_of([s1, s2, s3, one, one, one, base, base, x, x, y])
        stacked = jnp.concatenate([hi, hi, lo, parts, jnp.zeros((48, OBS), BF16)], axis=0)
        lhsx[pl.ds(pl.multiple_of((place - W) * OBS, OBS), OBS), :] = stacked.T

    def set_right(place, members, crd):
        hi, lo = split(members * ENS_SCALE)
        s1, s2, s3, base, x, y = position_parts(crd, place)
        one = jnp.ones((1, OBS), F32)
        parts = rows_of([one, one, one, s1, s2, s3, -2.0 * base, -2.0 * x, -2.0 * base, -2.0 * x, -2.0 * y])
        rhs[place, 0:64, 0:128] = hi
        rhs[place, 64:128, 0:128] = lo
        rhs[place, 128:192, 0:128] = hi
        rhs[place, 192:256, 0:128] = jnp.zeros((64, OBS), BF16)
        rhs[place, 0:192, 128:256] = jnp.zeros((192, OBS), BF16)
        rhs[place, 192:208, 128:256] = parts
        rhs[place, 208:256, 128:256] = jnp.zeros((48, OBS), BF16)

    def prepare_own(i, carry):
        members = ens_v[i]
        vectors = v_v[i]
        set_left(i + W, members, crd_v[i])
        set_right(i + W, members, crd_v[i])
        set_vectors(i + W, vectors)
        zf[0:16, lanes(i)] = vectors
        zf[16:32, lanes(i)] = obs_v[pl.ds(i, 1), :] * vectors
        return carry

    lax.fori_loop(0, NB, prepare_own, 0)

    def tiles(b, start, stop, mask):
        count = stop - start
        here = pl.ds(pl.multiple_of((b + start - W) * OBS, OBS), count * OBS)
        every = jnp.dot(lhsx[here, :], rhs[b], preferred_element_type=F32)
        for j in range(start, stop):
            both = every[(j - start) * OBS : (j - start + 1) * OBS]
            shared = both[:, 0:128]
            square = both[:, 128:256]
            inverse = lax.rsqrt(jnp.maximum(square, 1e-30))
            value = jnp.exp2(square * C_CORR * inverse) + jnp.exp2(square * C_LOC) * shared
            hi, lo = split(value * mask(b, j))
            kmat[b, j * OBS : (j + 1) * OBS, 0:128] = hi
            kmat[b, j * OBS : (j + 1) * OBS, 128:256] = lo

    def own_mask(b, j):
        return maskx[j + W, pl.ds(b - W, 1), :]

    def low_mask(b, j):
        return maskx[W - j, b + j - W : b + j - W + 1, :]

    def add(row, place, count, part):
        part = part[0:16] + part[16:32]
        zf[row : row + 16, lanes(place - W, count)] += part * STATIC_VAR

    def gather(b, start, stop, row):
        vectors = zx[row : row + 32, lanes(b + start, stop - start)]
        if row and start == 0:
            vectors = half_first(vectors)
        part = jnp.dot(
            vectors, kmat[b, start * OBS : stop * OBS, :],
            preferred_element_type=F32,
        )
        add(row // 2 + 16, b, 1, part[:, 0:128] + part[:, 128:256])

    def scatter(b, start, stop, row):
        vectors = zx[row : row + 32, lanes(b)]
        part = lax.dot_general(
            jnp.concatenate([vectors, vectors], axis=1), kmat[b, start * OBS : stop * OBS, :],
            (((1,), (1,)), ((), ())), preferred_element_type=F32,
        )
        if row and start == 0:
            part = half_first(part)
        add(row // 2 + 16, b + start, stop - start, part)

    last = NB

    def apply_to(b, inside):
        gather(b, 0, inside, 0)
        if inside > 1:
            scatter(b, 1, inside, 0)

    def step(b, carry):
        apply_to(b - 1, HALF)
        tiles(b, 0, HALF, own_mask)
        return carry

    tiles(W, 0, HALF, own_mask)
    lax.fori_loop(W + 1, 2 * W + EARLY, step, 0)
    tiles(last - W, W, HALF, own_mask)
    apply_to(2 * W + EARLY - 1, HALF)
    for b in range(last - W + 1, last):
        tiles(b, last - b, HALF, own_mask)
        scatter(b - 1, last + 1 - b, HALF, 0)
    tiles(last, 0, W, own_mask)
    scatter(last - 1, 1, HALF, 0)
    for b in range(last + 1, last + W):
        tiles(b, 0, last + W - b, own_mask)
        apply_to(b - 1, last + W + 1 - b)
    apply_to(last + W - 1, 1)

    for copy in small:
        copy.wait()
    for q in range(W):
        set_vectors(q, v_lo[q])
        set_vectors(q + NB + W, v_hi[q])
    for q in range(W):
        for copy in blocks[q]:
            copy.wait()
        low, high = W - 1 - q, last + W + q
        set_right(low, ens_lo[low], crd_lo[low])
        set_left(high, ens_hi[q], crd_hi[q])
        tiles(low, q + 1, HALF, low_mask)
        for j in range(q + 1, HALF):
            tiles(high - j, j, j + 1, own_mask)
        scatter(low, q + 1, HALF, 0)
        for j in range(q + 1, HALF):
            gather(high - j, j, j + 1, 0)

    moving = [
        remote(zf.at[16:32, 0 : W * OBS], p_hi, 12, left),
        remote(zf.at[16:32, (NB - W) * OBS : NB * OBS], p_lo, 13, right),
    ]
    for copy in moving:
        copy.start()

    tiles(2 * W + EARLY, 0, HALF, own_mask)
    lax.fori_loop(2 * W + EARLY + 1, last - W, step, 0)
    tiles(last - W, 0, W, own_mask)
    apply_to(last - W - 1, HALF)
    for b in range(last - W + 1, last):
        tiles(b, 0, last - b, own_mask)
        gather(b - 1, 0, HALF, 0)
        scatter(b - 1, 1, last + 1 - b, 0)
    gather(last - 1, 0, HALF, 0)

    def renew(row, source, start):
        hi, lo = split(source)
        zx[row : row + 16, start * OBS : start * OBS + source.shape[1]] = hi
        zx[row + 16 : row + 32, start * OBS : start * OBS + source.shape[1]] = lo

    renew(32, zf[16:32, :], W)

    def upper(b):
        zf[32:48, lanes(b - W)] = 0.5 * obs_v[pl.ds(b - W, 1), :] * zf[16:32, lanes(b - W)]
        gather(b, 0, HALF, 32)

    def uppers(i, carry):
        for more in range(UNROLL):
            upper(W + i * UNROLL + more)
        return carry

    lax.fori_loop(0, (last - W) // UNROLL, uppers, 0)
    for b in range(last, last + W):
        upper_lanes = lanes(b - W)
        zf[32:48, upper_lanes] = 0.5 * obs_v[b - W : b - W + 1, :] * zf[16:32, upper_lanes]
        gather(b, 0, last + W - b, 32)
    lane = lax.broadcasted_iota(jnp.int32, (16, OBS), 1)
    lane8 = lax.broadcasted_iota(jnp.int32, (8, OBS), 1)

    def turn(value, by):
        return pltpu.roll(value, by % OBS, 1)

    def columns_gram(row, row_end, col, col_end, inner):
        value = lax.dot_general(
            zx[row:row_end, inner], zx[col:col_end, inner], (((1,), (1,)), ((), ())), preferred_element_type=F32
        )
        if col:
            value = jnp.concatenate([jnp.zeros((row_end - row, col), F32), value], axis=1)
        return jnp.concatenate([value, jnp.zeros((row_end - row, OBS - col_end), F32)], axis=1)

    def fold(value):
        value = value[0:16] + value[16:32]
        return value + turn(value, -16)

    renew(64, zf[32:48, 0 : (NB - W) * OBS], W)
    known = columns_gram(0, 64, 0, 64, slice(W * OBS, (W + NB) * OBS))
    of_r = fold(known[0:32])
    first_gram = known[32:64] + columns_gram(32, 64, 64, 96, slice(W * OBS, last * OBS))
    even = (lane & 16) == 0
    for copy in moving:
        copy.wait()
    renew(32, p_hi[...], NB + W)
    for b in range(last, last + W):
        gather(b, last + W - b, HALF, 32)
    renew(64, zf[32:48, (NB - W) * OBS :], last)

    late = slice(last * OBS, (last + W) * OBS)
    total = first_gram + columns_gram(32, 64, 64, 96, late)
    own_part = jnp.where(even, of_r, turn(fold(total), -16))
    part_a[...] = jnp.where(lane8 < 64, own_part[0:8], turn(own_part[8:16], 64))

    def exchange(part, red, peer, send, recv):
        copies = [
            pltpu.make_async_remote_copy(
                src_ref=part, dst_ref=red.at[step - 1], send_sem=send.at[step - 1], recv_sem=recv.at[step - 1],
                device_id=peer(step), device_id_type=MESH,
            )
            for step in range(1, 16)
        ]
        for copy in copies:
            copy.start()
        return copies

    first_sum = exchange(part_a, red_a, peer_a, send_a, recv_a)

    def rest(i, carry):
        for more in range(UNROLL):
            scatter(W + i * UNROLL + more, 0, HALF, 32)
        return carry

    renew(32, p_lo[...], 0)
    for b in range(W):
        scatter(b, W - b, HALF, 32)
    lax.fori_loop(0, (last - W) // UNROLL, rest, 0)
    for b in range(last, last + W):
        scatter(b, 0, last + W - b, 32)

    def other_half(i, carry):
        zf[32:48, lanes(i)] += 0.5 * obs_v[pl.ds(i, 1), :] * zf[16:32, lanes(i)]
        return carry

    lax.fori_loop(0, NB, other_half, 0)
    for copy in first_sum:
        copy.wait()
    part_b[...] = part_a[...] + jnp.sum(red_a[...], axis=0)
    second_sum = exchange(part_b, red_b, peer_b, send_b, recv_b)
    for copy in second_sum:
        copy.wait()
    packed = part_b[...] + jnp.sum(red_b[...], axis=0)

    moments = jnp.concatenate([packed, turn(packed, 64)], axis=0)
    top = jnp.where(lane < 16, turn(moments, -32), jnp.where(lane < 32, moments, turn(moments, 32)))
    low = jnp.where(lane < 16, turn(moments, -16), jnp.where(lane < 32, turn(moments, -32), moments))
    system = jnp.concatenate([top, low], axis=0)
    rows = lax.broadcasted_iota(jnp.int32, (32, OBS), 0)
    half = jnp.where((lane >= 16) & (lane < 32), system[16:32], 0.0)
    flipped = jnp.concatenate([half, jnp.zeros((112, OBS), F32)], axis=0).T[16:32, :]
    system = jnp.concatenate([system[0:16], system[16:32] + turn(flipped, 16)], axis=0)
    spread = [jnp.broadcast_to(system[:, j : j + 1], (32, OBS)) for j in range(32)]
    inverses = []
    for k in range(32):
        inverse = 1.0 / spread[k][k : k + 1, :]
        factor = jnp.where(rows == k, 0.0, spread[k] * inverse)
        for j in range(k + 1, 32):
            spread[j] = spread[j] - factor * spread[j][k : k + 1, :]
        system = system - factor * system[k : k + 1, :]
        inverses.append(inverse)
    system = system * jnp.concatenate(inverses, axis=0)

    solved = jnp.concatenate([system, jnp.zeros((96, OBS), F32)], axis=0).T
    for_w = jnp.where(lane < 32, solved[32:48, :], 0.0)
    both = jnp.concatenate([for_w, turn(for_w, 16)], axis=0)[:, 0:48]
    for chunk in range(4):
        here = slice(chunk * 4 * OBS, (chunk + 1) * 4 * OBS)
        sums = jnp.dot(both, zf[:, here], preferred_element_type=F32, precision=lax.Precision.HIGHEST)
        left_over = zf[0:16, here] - sums[16:32]
        for piece in range(4):
            b = chunk * 4 + piece
            w_out[b] = sums[0:16, piece * OBS : (piece + 1) * OBS]
            r_out[b] = left_over[:, piece * OBS : (piece + 1) * OBS]


def on_device(innovations, ensemble, coords, obs_error, pair_cols, pair_count):
    del pair_count
    vmem = pl.BlockSpec(memory_space=pltpu.VMEM)
    arrays = [pltpu.with_memory_space_constraint(a, pltpu.HBM) for a in (innovations, ensemble, coords, obs_error, pair_cols)]
    out = jax.ShapeDtypeStruct((NB, RHS, OBS), F32)
    return pl.pallas_call(
        kernel,
        out_shape=(out, out),
        in_specs=[pl.BlockSpec(memory_space=pltpu.HBM)] * 5,
        out_specs=(vmem, vmem),
        scratch_shapes=[
            pltpu.VMEM((NB, MEM, OBS), F32),
            pltpu.VMEM((NB, 2, OBS), jnp.int32),
            pltpu.VMEM((NB, RHS, OBS), F32),
            pltpu.VMEM((NB, OBS), F32),
            pltpu.VMEM((NB, SLOTS), jnp.int32),
            pltpu.VMEM(((NB + W) * OBS, 256), BF16),
            pltpu.VMEM((NB + W, 256, 256), BF16),
            pltpu.VMEM((NB + W, HALF * OBS, 256), BF16),
            pltpu.VMEM((96, NX * OBS), BF16),
            pltpu.VMEM((48, NB * OBS), F32),
            pltpu.VMEM((SLOTS, NB, OBS), F32),
            pltpu.VMEM((W, MEM, OBS), F32),
            pltpu.VMEM((W, MEM, OBS), F32),
            pltpu.VMEM((W, 2, OBS), jnp.int32),
            pltpu.VMEM((W, 2, OBS), jnp.int32),
            pltpu.VMEM((W, RHS, OBS), F32),
            pltpu.VMEM((W, RHS, OBS), F32),
            pltpu.VMEM((RHS, W * OBS), F32),
            pltpu.VMEM((RHS, W * OBS), F32),
            pltpu.VMEM((8, OBS), F32),
            pltpu.VMEM((8, OBS), F32),
            pltpu.VMEM((15, 8, OBS), F32),
            pltpu.VMEM((15, 8, OBS), F32),
            pltpu.SemaphoreType.DMA((5,)),
            pltpu.SemaphoreType.DMA((14,)),
            pltpu.SemaphoreType.DMA((14,)),
            pltpu.SemaphoreType.DMA((15,)),
            pltpu.SemaphoreType.DMA((15,)),
            pltpu.SemaphoreType.DMA((15,)),
            pltpu.SemaphoreType.DMA((15,)),
        ],
        compiler_params=pltpu.CompilerParams(
            collective_id=0, has_side_effects=True, vmem_limit_bytes=LIMIT
        ),
    )(*arrays)


def solution(mesh):
    both = ("region", "sub")
    in_specs = (
        P(both, None, None),
        P(both, None, None),
        P(both, None, None),
        P(both, None),
        P(both, None),
        P(both),
    )
    out_specs = (P(both, None, None), P(both, None, None))
    return jax.shard_map(on_device, mesh=mesh, in_specs=in_specs, out_specs=out_specs, check_vma=False)
```

```python
import jax
import jax.numpy as jnp
from jax import lax
from jax.experimental import pallas as pl
from jax.experimental.pallas import tpu as pltpu
from jax.sharding import PartitionSpec as P

MESH = pl.DeviceIdType.MESH
F32 = jnp.float32
BF16 = jnp.bfloat16

LIMIT = 40 * 1024 * 1024
UNROLL = 4
EARLY = 3
NB = 16
W = 4
NX = NB + 2 * W
SLOTS = 2 * W + 1
HALF = W + 1
OBS = 128
RHS = 16
MEM = 64

STATIC_VAR = 0.002
LOG2E = 1.4426950408889634
C_CORR = -LOG2E / 150.0
C_LOC = -LOG2E / (2.0 * 200.0**2)
ENS_SCALE = 1.0 / ((MEM - 1) * STATIC_VAR)


def split(value):
    hi = value.astype(BF16)
    lo = (value - hi.astype(F32)).astype(BF16)
    return hi, lo


def half_first(value):
    first = value[:, 0:OBS] * 0.5
    return first if value.shape[1] == OBS else jnp.concatenate([first, value[:, OBS:]], axis=1)


def rows_of(rows):
    ids = lax.broadcasted_iota(jnp.int32, (16, OBS), 0)
    out = jnp.zeros((16, OBS), F32)
    for place, row in enumerate(rows):
        out = jnp.where(ids == place, jnp.broadcast_to(row, (16, OBS)), out)
    return out.astype(BF16)


def position_parts(crd, place):
    x = crd[0:1, :].astype(F32)
    y = crd[1:2, :].astype(F32)
    base = jnp.full((1, OBS), jnp.asarray(place - NX // 2).astype(F32) * 64.0, F32)
    full = x + base
    square = full * full + y * y
    s1 = square.astype(BF16).astype(F32)
    s2 = (square - s1).astype(BF16).astype(F32)
    s3 = square - s1 - s2
    return s1, s2, s3, base, x, y


def kernel(
    innov, ens, coords, obs, cols, w_out, r_out,
    ens_v, crd_v, v_v, obs_v, cols_v,
    lhsx, rhs, kmat, zx, zf, maskx,
    ens_lo, ens_hi, crd_lo, crd_hi, v_lo, v_hi, p_lo, p_hi,
    part_a, part_b, red_a, red_b,
    load_sem, halo_send, halo_recv, send_a, recv_a, send_b, recv_b,
):
    me = lax.axis_index("region") * 4 + lax.axis_index("sub")

    def device(index):
        return (lax.div(index, 4), lax.rem(index, 4))

    left = device(lax.rem(me + 255, 256))
    right = device(lax.rem(me + 1, 256))
    x = lax.rem(me, 4)
    core = lax.rem(lax.div(me, 4), 2)
    y = lax.rem(lax.div(me, 8), 4)
    z = lax.div(me, 32)

    def peer_a(step):
        there = lax.rem(y * 4 + x + step, 16)
        return device(((z * 4 + lax.div(there, 4)) * 2 + core) * 4 + lax.rem(there, 4))

    def peer_b(step):
        there = lax.rem(z * 2 + core + step, 16)
        return device(((lax.div(there, 2) * 4 + y) * 2 + lax.rem(there, 2)) * 4 + x)

    loads = [
        pltpu.make_async_copy(source, target, load_sem.at[i])
        for i, (source, target) in enumerate(
            ((cols, cols_v), (coords, crd_v), (ens, ens_v), (innov, v_v), (obs, obs_v))
        )
    ]
    for load in loads:
        load.start()
    barrier = pltpu.get_barrier_semaphore()
    for there in (left, right):
        pl.semaphore_signal(barrier, inc=1, device_id=there, device_id_type=MESH)

    for step in range(1, 16):
        pl.semaphore_signal(barrier, inc=1, device_id=peer_a(step), device_id_type=MESH)
        pl.semaphore_signal(barrier, inc=1, device_id=peer_b(step), device_id_type=MESH)
    pl.semaphore_wait(barrier, 32)

    def remote(src, dst, slot, there):
        return pltpu.make_async_remote_copy(
            src_ref=src, dst_ref=dst, send_sem=halo_send.at[slot], recv_sem=halo_recv.at[slot],
            device_id=there, device_id_type=MESH,
        )

    small = [
        remote(coords.at[NB - W : NB], crd_lo, 0, right),
        remote(coords.at[0:W], crd_hi, 1, left),
        remote(innov.at[NB - W : NB], v_lo, 2, right),
        remote(innov.at[0:W], v_hi, 3, left),
    ]
    blocks = [
        (
            remote(ens.at[NB - 1 - q], ens_lo.at[W - 1 - q], 4 + 2 * q, right),
            remote(ens.at[q], ens_hi.at[q], 5 + 2 * q, left),
        )
        for q in range(W)
    ]
    for copy in small:
        copy.start()
    for pair in blocks:
        for copy in pair:
            copy.start()
    for load in loads:
        load.wait()

    offset = cols_v[...] - (lax.broadcasted_iota(jnp.int32, (NB, SLOTS), 0) + me * NB)
    for slot in range(SLOTS):
        hit = jnp.max(jnp.where(offset == slot - W, 1.0, 0.0).astype(F32), axis=1, keepdims=True)
        maskx[slot] = jnp.broadcast_to(hit, (NB, OBS))

    def lanes(place, count=1):
        return pl.ds(pl.multiple_of(place * OBS, OBS), count * OBS)

    def set_vectors(place, vectors):
        hi, lo = split(vectors)
        zx[0:16, lanes(place)] = hi
        zx[16:32, lanes(place)] = lo

    def set_left(place, members, crd):
        hi, lo = split(members)
        s1, s2, s3, base, x, y = position_parts(crd, place)
        one = jnp.ones((1, OBS), F32)
        parts = rows_of([s1, s2, s3, one, one, one, base, base, x, x, y])
        stacked = jnp.concatenate([hi, hi, lo, parts, jnp.zeros((48, OBS), BF16)], axis=0)
        lhsx[pl.ds(pl.multiple_of((place - W) * OBS, OBS), OBS), :] = stacked.T

    def set_right(place, members, crd):
        hi, lo = split(members * ENS_SCALE)
        s1, s2, s3, base, x, y = position_parts(crd, place)
        one = jnp.ones((1, OBS), F32)
        parts = rows_of([one, one, one, s1, s2, s3, -2.0 * base, -2.0 * x, -2.0 * base, -2.0 * x, -2.0 * y])
        rhs[place, 0:64, 0:128] = hi
        rhs[place, 64:128, 0:128] = lo
        rhs[place, 128:192, 0:128] = hi
        rhs[place, 192:256, 0:128] = jnp.zeros((64, OBS), BF16)
        rhs[place, 0:192, 128:256] = jnp.zeros((192, OBS), BF16)
        rhs[place, 192:208, 128:256] = parts
        rhs[place, 208:256, 128:256] = jnp.zeros((48, OBS), BF16)

    def prepare_own(i, carry):
        members = ens_v[i]
        vectors = v_v[i]
        set_left(i + W, members, crd_v[i])
        set_right(i + W, members, crd_v[i])
        set_vectors(i + W, vectors)
        zf[0:16, lanes(i)] = vectors
        zf[16:32, lanes(i)] = obs_v[pl.ds(i, 1), :] * vectors
        return carry

    lax.fori_loop(0, NB, prepare_own, 0)

    def tiles(b, start, stop, mask):
        count = stop - start
        here = pl.ds(pl.multiple_of((b + start - W) * OBS, OBS), count * OBS)
        every = jnp.dot(lhsx[here, :], rhs[b], preferred_element_type=F32)
        for j in range(start, stop):
            both = every[(j - start) * OBS : (j - start + 1) * OBS]
            shared = both[:, 0:128]
            square = both[:, 128:256]
            inverse = lax.rsqrt(jnp.maximum(square, 1e-30))
            value = jnp.exp2(square * C_CORR * inverse) + jnp.exp2(square * C_LOC) * shared
            hi, lo = split(value * mask(b, j))
            kmat[b, j * OBS : (j + 1) * OBS, 0:128] = hi
            kmat[b, j * OBS : (j + 1) * OBS, 128:256] = lo

    def own_mask(b, j):
        return maskx[j + W, pl.ds(b - W, 1), :]

    def low_mask(b, j):
        return maskx[W - j, b + j - W : b + j - W + 1, :]

    def add(row, place, count, part):
        part = part[0:16] + part[16:32]
        zf[row : row + 16, lanes(place - W, count)] += part * STATIC_VAR

    def gather(b, start, stop, row):
        vectors = zx[row : row + 32, lanes(b + start, stop - start)]
        if row and start == 0:
            vectors = half_first(vectors)
        part = jnp.dot(
            vectors, kmat[b, start * OBS : stop * OBS, :],
            preferred_element_type=F32,
        )
        add(row // 2 + 16, b, 1, part[:, 0:128] + part[:, 128:256])

    def scatter(b, start, stop, row):
        vectors = zx[row : row + 32, lanes(b)]
        part = lax.dot_general(
            jnp.concatenate([vectors, vectors], axis=1), kmat[b, start * OBS : stop * OBS, :],
            (((1,), (1,)), ((), ())), preferred_element_type=F32,
        )
        if row and start == 0:
            part = half_first(part)
        add(row // 2 + 16, b + start, stop - start, part)

    last = NB

    def apply_to(b, inside):
        gather(b, 0, inside, 0)
        if inside > 1:
            scatter(b, 1, inside, 0)

    def step(b, carry):
        apply_to(b - 1, HALF)
        tiles(b, 0, HALF, own_mask)
        return carry

    tiles(W, 0, HALF, own_mask)
    lax.fori_loop(W + 1, 2 * W + EARLY, step, 0)
    tiles(last - W, W, HALF, own_mask)
    apply_to(2 * W + EARLY - 1, HALF)
    for b in range(last - W + 1, last):
        tiles(b, last - b, HALF, own_mask)
        scatter(b - 1, last + 1 - b, HALF, 0)
    tiles(last, 0, W, own_mask)
    scatter(last - 1, 1, HALF, 0)
    for b in range(last + 1, last + W):
        tiles(b, 0, last + W - b, own_mask)
        apply_to(b - 1, last + W + 1 - b)
    apply_to(last + W - 1, 1)

    small[0].wait()
    small[2].wait()
    for q in range(W):
        set_vectors(q, v_lo[q])
    for q in range(W):
        low = W - 1 - q
        blocks[q][0].wait()
        set_right(low, ens_lo[low], crd_lo[low])
        tiles(low, q + 1, HALF, low_mask)
        if q:
            scatter(low + 1, q, HALF, 0)
    scatter(0, W, HALF, 0)
    to_left = remote(zf.at[16:32, 0 : W * OBS], p_hi, 12, left)
    to_left.start()

    small[1].wait()
    small[3].wait()
    for q in range(W):
        set_vectors(q + NB + W, v_hi[q])
    for q in range(W):
        high = last + W + q
        blocks[q][1].wait()
        set_left(high, ens_hi[q], crd_hi[q])
        for j in range(q + 1, HALF):
            tiles(high - j, j, j + 1, own_mask)
    for b in range(last, last + W):
        gather(b, last + W - b, HALF, 0)
    to_right = remote(zf.at[16:32, (NB - W) * OBS : NB * OBS], p_lo, 13, right)
    to_right.start()

    tiles(2 * W + EARLY, 0, HALF, own_mask)
    lax.fori_loop(2 * W + EARLY + 1, last - W, step, 0)
    tiles(last - W, 0, W, own_mask)
    apply_to(last - W - 1, HALF)
    for b in range(last - W + 1, last):
        tiles(b, 0, last - b, own_mask)
        gather(b - 1, 0, HALF, 0)
        scatter(b - 1, 1, last + 1 - b, 0)
    gather(last - 1, 0, HALF, 0)

    def renew(row, source, start):
        hi, lo = split(source)
        zx[row : row + 16, start * OBS : start * OBS + source.shape[1]] = hi
        zx[row + 16 : row + 32, start * OBS : start * OBS + source.shape[1]] = lo

    renew(32, zf[16:32, :], W)

    def upper(b):
        zf[32:48, lanes(b - W)] = 0.5 * obs_v[pl.ds(b - W, 1), :] * zf[16:32, lanes(b - W)]
        gather(b, 0, HALF, 32)

    def uppers(i, carry):
        for more in range(UNROLL):
            upper(W + i * UNROLL + more)
        return carry

    lax.fori_loop(0, (last - W) // UNROLL, uppers, 0)
    for b in range(last, last + W):
        upper_lanes = lanes(b - W)
        zf[32:48, upper_lanes] = 0.5 * obs_v[b - W : b - W + 1, :] * zf[16:32, upper_lanes]
        gather(b, 0, last + W - b, 32)
    lane = lax.broadcasted_iota(jnp.int32, (16, OBS), 1)
    lane8 = lax.broadcasted_iota(jnp.int32, (8, OBS), 1)

    def turn(value, by):
        return pltpu.roll(value, by % OBS, 1)

    def product_gram(left_rows, right_rows):
        value = lax.dot_general(left_rows, right_rows, (((1,), (1,)), ((), ())), preferred_element_type=F32)
        height, width = value.shape
        value = jnp.concatenate([value, jnp.zeros((height, OBS - width), F32)], axis=1)
        value = value[0:16] + value[16:32] if height == 32 else value
        return value + turn(value, -16) if height == 32 else value

    own = slice(W * OBS, (W + NB) * OBS)
    renew(64, zf[32:48, :], W)
    of_r = product_gram(zx[0:32, own], zx[0:64, own])
    of_p = product_gram(zx[32:64, own], zx[32:96, own])
    of_h = product_gram(zx[64:96, own], zx[32:64, own])
    place = lane >> 4
    early = jnp.where(
        place == 0, of_r, jnp.where(place == 1, turn(of_p, 16), jnp.where(place == 2, of_r, turn(of_p, 16) + turn(of_h, 48)))
    )
    across = [None] * W
    for b in range(last, last + W):
        start = last + W - b
        vectors = zx[32:64, b * OBS : (b + 1) * OBS]
        part = lax.dot_general(
            jnp.concatenate([vectors, vectors], axis=1), kmat[b, start * OBS :, :],
            (((1,), (1,)), ((), ())), preferred_element_type=F32,
        )
        part = (part[0:16] + part[16:32]) * STATIC_VAR
        for i in range(HALF - start):
            piece = part[:, i * OBS : (i + 1) * OBS]
            across[i] = piece if across[i] is None else across[i] + piece
    across = jnp.concatenate(split(jnp.concatenate(across, axis=1)), axis=0)
    to_left.wait()
    theirs = jnp.concatenate(split(p_hi[...]), axis=0)
    late = product_gram(across, theirs) + product_gram(theirs, across)
    own_part = jnp.where(place == 3, early + turn(late, 48), early)
    part_a[...] = jnp.where(lane8 < 64, own_part[0:8], turn(own_part[8:16], 64))

    def exchange(part, red, peer, send, recv):
        copies = [
            pltpu.make_async_remote_copy(
                src_ref=part, dst_ref=red.at[step - 1], send_sem=send.at[step - 1], recv_sem=recv.at[step - 1],
                device_id=peer(step), device_id_type=MESH,
            )
            for step in range(1, 16)
        ]
        for copy in copies:
            copy.start()
        return copies

    first_sum = exchange(part_a, red_a, peer_a, send_a, recv_a)

    def rest(i, carry):
        for more in range(UNROLL):
            scatter(W + i * UNROLL + more, 0, HALF, 32)
        return carry

    renew(32, p_hi[...], NB + W)
    for b in range(last, last + W):
        gather(b, last + W - b, HALF, 32)
    to_right.wait()
    renew(32, p_lo[...], 0)
    for b in range(W):
        scatter(b, W - b, HALF, 32)
    lax.fori_loop(0, (last - W) // UNROLL, rest, 0)
    for b in range(last, last + W):
        scatter(b, 0, last + W - b, 32)

    def other_half(i, carry):
        zf[32:48, lanes(i)] += 0.5 * obs_v[pl.ds(i, 1), :] * zf[16:32, lanes(i)]
        return carry

    lax.fori_loop(0, NB, other_half, 0)
    for copy in first_sum:
        copy.wait()
    part_b[...] = part_a[...] + jnp.sum(red_a[...], axis=0)
    second_sum = exchange(part_b, red_b, peer_b, send_b, recv_b)
    for copy in second_sum:
        copy.wait()
    packed = part_b[...] + jnp.sum(red_b[...], axis=0)

    moments = jnp.concatenate([packed, turn(packed, 64)], axis=0)
    rows = lax.broadcasted_iota(jnp.int32, (32, OBS), 0)

    def column(at):
        return jnp.broadcast_to(moments[:, at : at + 1], (16, OBS))

    system = jnp.concatenate([moments, turn(moments, -32)], axis=0)
    middle = [column(16 + j) for j in range(16)]
    spread = [jnp.concatenate([column(32 + j), middle[j]], axis=0) for j in range(16)]
    spread += [jnp.concatenate([middle[j], column(48 + j)], axis=0) for j in range(16)]
    inverses = []
    for k in range(32):
        inverse = 1.0 / spread[k][k : k + 1, :]
        factor = jnp.where(rows == k, 0.0, spread[k] * inverse)
        for j in range(k + 1, 32):
            spread[j] = spread[j] - factor * spread[j][k : k + 1, :]
        system = system - factor * system[k : k + 1, :]
        inverses.append(inverse)
    system = system * jnp.concatenate(inverses, axis=0)

    solved = jnp.concatenate([system, jnp.zeros((96, OBS), F32)], axis=0).T
    for_w = jnp.where(lane < 32, solved[0:16, :], 0.0)
    both = jnp.concatenate([for_w, turn(for_w, 16)], axis=0)[:, 0:48]
    for chunk in range(4):
        here = slice(chunk * 4 * OBS, (chunk + 1) * 4 * OBS)
        sums = jnp.dot(both, zf[:, here], preferred_element_type=F32, precision=lax.Precision.HIGHEST)
        left_over = zf[0:16, here] - sums[16:32]
        for piece in range(4):
            b = chunk * 4 + piece
            w_out[b] = sums[0:16, piece * OBS : (piece + 1) * OBS]
            r_out[b] = left_over[:, piece * OBS : (piece + 1) * OBS]


def on_device(innovations, ensemble, coords, obs_error, pair_cols, pair_count):
    del pair_count
    vmem = pl.BlockSpec(memory_space=pltpu.VMEM)
    arrays = [pltpu.with_memory_space_constraint(a, pltpu.HBM) for a in (innovations, ensemble, coords, obs_error, pair_cols)]
    out = jax.ShapeDtypeStruct((NB, RHS, OBS), F32)
    return pl.pallas_call(
        kernel,
        out_shape=(out, out),
        in_specs=[pl.BlockSpec(memory_space=pltpu.HBM)] * 5,
        out_specs=(vmem, vmem),
        scratch_shapes=[
            pltpu.VMEM((NB, MEM, OBS), F32),
            pltpu.VMEM((NB, 2, OBS), jnp.int32),
            pltpu.VMEM((NB, RHS, OBS), F32),
            pltpu.VMEM((NB, OBS), F32),
            pltpu.VMEM((NB, SLOTS), jnp.int32),
            pltpu.VMEM(((NB + W) * OBS, 256), BF16),
            pltpu.VMEM((NB + W, 256, 256), BF16),
            pltpu.VMEM((NB + W, HALF * OBS, 256), BF16),
            pltpu.VMEM((96, NX * OBS), BF16),
            pltpu.VMEM((48, NB * OBS), F32),
            pltpu.VMEM((SLOTS, NB, OBS), F32),
            pltpu.VMEM((W, MEM, OBS), F32),
            pltpu.VMEM((W, MEM, OBS), F32),
            pltpu.VMEM((W, 2, OBS), jnp.int32),
            pltpu.VMEM((W, 2, OBS), jnp.int32),
            pltpu.VMEM((W, RHS, OBS), F32),
            pltpu.VMEM((W, RHS, OBS), F32),
            pltpu.VMEM((RHS, W * OBS), F32),
            pltpu.VMEM((RHS, W * OBS), F32),
            pltpu.VMEM((8, OBS), F32),
            pltpu.VMEM((8, OBS), F32),
            pltpu.VMEM((15, 8, OBS), F32),
            pltpu.VMEM((15, 8, OBS), F32),
            pltpu.SemaphoreType.DMA((5,)),
            pltpu.SemaphoreType.DMA((14,)),
            pltpu.SemaphoreType.DMA((14,)),
            pltpu.SemaphoreType.DMA((15,)),
            pltpu.SemaphoreType.DMA((15,)),
            pltpu.SemaphoreType.DMA((15,)),
            pltpu.SemaphoreType.DMA((15,)),
        ],
        compiler_params=pltpu.CompilerParams(
            collective_id=0, has_side_effects=True, vmem_limit_bytes=LIMIT
        ),
    )(*arrays)


def solution(mesh):
    both = ("region", "sub")
    in_specs = (
        P(both, None, None),
        P(both, None, None),
        P(both, None, None),
        P(both, None),
        P(both, None),
        P(both),
    )
    out_specs = (P(both, None, None), P(both, None, None))
    return jax.shard_map(on_device, mesh=mesh, in_specs=in_specs, out_specs=out_specs, check_vma=False)
```

```python
import jax
import jax.numpy as jnp
from jax import lax
from jax.experimental import pallas as pl
from jax.experimental.pallas import tpu as pltpu
from jax.sharding import PartitionSpec as P

MESH = pl.DeviceIdType.MESH
F32 = jnp.float32
BF16 = jnp.bfloat16

LIMIT = 40 * 1024 * 1024
UNROLL = 4
EARLY = 3
NB = 16
W = 4
NX = NB + 2 * W
SLOTS = 2 * W + 1
HALF = W + 1
OBS = 128
RHS = 16
MEM = 64

STATIC_VAR = 0.002
LOG2E = 1.4426950408889634
C_CORR = -LOG2E / 150.0
C_LOC = -LOG2E / (2.0 * 200.0**2)
ENS_SCALE = 1.0 / ((MEM - 1) * STATIC_VAR)


def split(value):
    hi = value.astype(BF16)
    lo = (value - hi.astype(F32)).astype(BF16)
    return hi, lo


def half_first(value):
    first = value[:, 0:OBS] * 0.5
    return first if value.shape[1] == OBS else jnp.concatenate([first, value[:, OBS:]], axis=1)


def rows_of(rows):
    ids = lax.broadcasted_iota(jnp.int32, (16, OBS), 0)
    out = jnp.zeros((16, OBS), F32)
    for place, row in enumerate(rows):
        out = jnp.where(ids == place, jnp.broadcast_to(row, (16, OBS)), out)
    return out.astype(BF16)


def position_parts(crd, place):
    x = crd[0:1, :].astype(F32)
    y = crd[1:2, :].astype(F32)
    base = jnp.full((1, OBS), jnp.asarray(place - NX // 2).astype(F32) * 64.0, F32)
    full = x + base
    square = full * full + y * y
    s1 = square.astype(BF16).astype(F32)
    s2 = (square - s1).astype(BF16).astype(F32)
    s3 = square - s1 - s2
    return s1, s2, s3, base, x, y


def kernel(
    innov, ens, coords, obs, cols, w_out, r_out,
    ens_v, crd_v, v_v, obs_v, cols_v,
    lhsx, rhs, kmat, zx, zf, maskx,
    ens_lo, ens_hi, crd_lo, crd_hi, v_lo, v_hi, p_lo, p_hi,
    part_a, part_b, red_a, red_b,
    load_sem, halo_send, halo_recv, send_a, recv_a, send_b, recv_b,
):
    me = lax.axis_index("region") * 4 + lax.axis_index("sub")

    def device(index):
        return (lax.div(index, 4), lax.rem(index, 4))

    left = device(lax.rem(me + 255, 256))
    right = device(lax.rem(me + 1, 256))
    x = lax.rem(me, 4)
    core = lax.rem(lax.div(me, 4), 2)
    y = lax.rem(lax.div(me, 8), 4)
    z = lax.div(me, 32)

    def peer_a(dy, dx):
        return device(((z * 4 + lax.rem(y + dy, 4)) * 2 + core) * 4 + lax.rem(x + dx, 4))

    def peer_b(dz, dc):
        return device(((lax.rem(z + dz, 8) * 4 + y) * 2 + lax.rem(core + dc, 2)) * 4 + x)

    peers_a = [peer_a(dy, dx) for dy, dx in sorted(
        ((dy, dx) for dy in range(4) for dx in range(4) if dy or dx),
        key=lambda by: -min(by[0], 4 - by[0]) - min(by[1], 4 - by[1]),
    )]
    peers_b = [peer_b(dz, dc) for dz, dc in sorted(
        ((dz, dc) for dz in range(8) for dc in range(2) if dz or dc),
        key=lambda by: -2 * min(by[0], 8 - by[0]) - by[1],
    )]

    loads = [
        pltpu.make_async_copy(source, target, load_sem.at[i])
        for i, (source, target) in enumerate(
            ((cols, cols_v), (coords, crd_v), (ens, ens_v), (innov, v_v), (obs, obs_v))
        )
    ]
    for load in loads:
        load.start()
    barrier = pltpu.get_barrier_semaphore()
    for there in (left, right):
        pl.semaphore_signal(barrier, inc=1, device_id=there, device_id_type=MESH)

    for there in peers_b + peers_a:
        pl.semaphore_signal(barrier, inc=1, device_id=there, device_id_type=MESH)
    pl.semaphore_wait(barrier, 32)

    def remote(src, dst, slot, there):
        return pltpu.make_async_remote_copy(
            src_ref=src, dst_ref=dst, send_sem=halo_send.at[slot], recv_sem=halo_recv.at[slot],
            device_id=there, device_id_type=MESH,
        )

    small = [
        remote(coords.at[NB - W : NB], crd_lo, 0, right),
        remote(coords.at[0:W], crd_hi, 1, left),
        remote(innov.at[NB - W : NB], v_lo, 2, right),
        remote(innov.at[0:W], v_hi, 3, left),
    ]
    blocks = [
        (
            remote(ens.at[NB - 1 - q], ens_lo.at[W - 1 - q], 4 + 2 * q, right),
            remote(ens.at[q], ens_hi.at[q], 5 + 2 * q, left),
        )
        for q in range(W)
    ]
    for copy in small:
        copy.start()
    for pair in blocks:
        for copy in pair:
            copy.start()
    for load in loads:
        load.wait()

    offset = cols_v[...] - (lax.broadcasted_iota(jnp.int32, (NB, SLOTS), 0) + me * NB)
    for slot in range(SLOTS):
        hit = jnp.max(jnp.where(offset == slot - W, 1.0, 0.0).astype(F32), axis=1, keepdims=True)
        maskx[slot] = jnp.broadcast_to(hit, (NB, OBS))

    def lanes(place, count=1):
        return pl.ds(pl.multiple_of(place * OBS, OBS), count * OBS)

    def set_vectors(place, vectors):
        hi, lo = split(vectors)
        zx[0:16, lanes(place)] = hi
        zx[16:32, lanes(place)] = lo

    def set_left(place, members, crd):
        hi, lo = split(members)
        s1, s2, s3, base, x, y = position_parts(crd, place)
        one = jnp.ones((1, OBS), F32)
        parts = rows_of([s1, s2, s3, one, one, one, base, base, x, x, y])
        stacked = jnp.concatenate([hi, hi, lo, parts, jnp.zeros((48, OBS), BF16)], axis=0)
        lhsx[pl.ds(pl.multiple_of((place - W) * OBS, OBS), OBS), :] = stacked.T

    def set_right(place, members, crd):
        hi, lo = split(members * ENS_SCALE)
        s1, s2, s3, base, x, y = position_parts(crd, place)
        one = jnp.ones((1, OBS), F32)
        parts = rows_of([one, one, one, s1, s2, s3, -2.0 * base, -2.0 * x, -2.0 * base, -2.0 * x, -2.0 * y])
        rhs[place, 0:64, 0:128] = hi
        rhs[place, 64:128, 0:128] = lo
        rhs[place, 128:192, 0:128] = hi
        rhs[place, 192:256, 0:128] = jnp.zeros((64, OBS), BF16)
        rhs[place, 0:192, 128:256] = jnp.zeros((192, OBS), BF16)
        rhs[place, 192:208, 128:256] = parts
        rhs[place, 208:256, 128:256] = jnp.zeros((48, OBS), BF16)

    def prepare_own(i, carry):
        members = ens_v[i]
        vectors = v_v[i]
        set_left(i + W, members, crd_v[i])
        set_right(i + W, members, crd_v[i])
        set_vectors(i + W, vectors)
        zf[0:16, lanes(i)] = vectors
        zf[16:32, lanes(i)] = obs_v[pl.ds(i, 1), :] * vectors
        return carry

    lax.fori_loop(0, NB, prepare_own, 0)

    def tiles(b, start, stop, mask):
        count = stop - start
        here = pl.ds(pl.multiple_of((b + start - W) * OBS, OBS), count * OBS)
        every = jnp.dot(lhsx[here, :], rhs[b], preferred_element_type=F32)
        for j in range(start, stop):
            both = every[(j - start) * OBS : (j - start + 1) * OBS]
            shared = both[:, 0:128]
            square = both[:, 128:256]
            inverse = lax.rsqrt(jnp.maximum(square, 1e-30))
            value = jnp.exp2(square * C_CORR * inverse) + jnp.exp2(square * C_LOC) * shared
            hi, lo = split(value * mask(b, j))
            kmat[b, j * OBS : (j + 1) * OBS, 0:128] = hi
            kmat[b, j * OBS : (j + 1) * OBS, 128:256] = lo

    def own_mask(b, j):
        return maskx[j + W, pl.ds(b - W, 1), :]

    def low_mask(b, j):
        return maskx[W - j, b + j - W : b + j - W + 1, :]

    def add(row, place, count, part):
        part = part[0:16] + part[16:32]
        zf[row : row + 16, lanes(place - W, count)] += part * STATIC_VAR

    def gather(b, start, stop, row):
        vectors = zx[row : row + 32, lanes(b + start, stop - start)]
        if row and start == 0:
            vectors = half_first(vectors)
        part = jnp.dot(
            vectors, kmat[b, start * OBS : stop * OBS, :],
            preferred_element_type=F32,
        )
        add(row // 2 + 16, b, 1, part[:, 0:128] + part[:, 128:256])

    def scatter(b, start, stop, row):
        vectors = zx[row : row + 32, lanes(b)]
        part = lax.dot_general(
            jnp.concatenate([vectors, vectors], axis=1), kmat[b, start * OBS : stop * OBS, :],
            (((1,), (1,)), ((), ())), preferred_element_type=F32,
        )
        if row and start == 0:
            part = half_first(part)
        add(row // 2 + 16, b + start, stop - start, part)

    last = NB

    def apply_to(b, inside):
        gather(b, 0, inside, 0)
        if inside > 1:
            scatter(b, 1, inside, 0)

    def step(b, carry):
        apply_to(b - 1, HALF)
        tiles(b, 0, HALF, own_mask)
        return carry

    tiles(W, 0, HALF, own_mask)
    lax.fori_loop(W + 1, 2 * W + EARLY, step, 0)
    tiles(last - W, W, HALF, own_mask)
    apply_to(2 * W + EARLY - 1, HALF)
    for b in range(last - W + 1, last):
        tiles(b, last - b, HALF, own_mask)
        scatter(b - 1, last + 1 - b, HALF, 0)
    tiles(last, 0, W, own_mask)
    scatter(last - 1, 1, HALF, 0)
    for b in range(last + 1, last + W):
        tiles(b, 0, last + W - b, own_mask)
        apply_to(b - 1, last + W + 1 - b)
    apply_to(last + W - 1, 1)

    small[0].wait()
    small[2].wait()
    for q in range(W):
        set_vectors(q, v_lo[q])
    for q in range(W):
        low = W - 1 - q
        blocks[q][0].wait()
        set_right(low, ens_lo[low], crd_lo[low])
        tiles(low, q + 1, HALF, low_mask)
        if q:
            scatter(low + 1, q, HALF, 0)
    scatter(0, W, HALF, 0)
    to_left = remote(zf.at[16:32, 0 : W * OBS], p_hi, 12, left)
    to_left.start()

    small[1].wait()
    small[3].wait()
    for q in range(W):
        set_vectors(q + NB + W, v_hi[q])
    for q in range(W):
        high = last + W + q
        blocks[q][1].wait()
        set_left(high, ens_hi[q], crd_hi[q])
        for j in range(q + 1, HALF):
            tiles(high - j, j, j + 1, own_mask)
    for b in range(last, last + W):
        gather(b, last + W - b, HALF, 0)
    to_right = remote(zf.at[16:32, (NB - W) * OBS : NB * OBS], p_lo, 13, right)
    to_right.start()

    tiles(2 * W + EARLY, 0, HALF, own_mask)
    lax.fori_loop(2 * W + EARLY + 1, last - W, step, 0)
    tiles(last - W, 0, W, own_mask)
    apply_to(last - W - 1, HALF)
    for b in range(last - W + 1, last):
        tiles(b, 0, last - b, own_mask)
        gather(b - 1, 0, HALF, 0)
        scatter(b - 1, 1, last + 1 - b, 0)
    gather(last - 1, 0, HALF, 0)

    def renew(row, source, start):
        hi, lo = split(source)
        zx[row : row + 16, start * OBS : start * OBS + source.shape[1]] = hi
        zx[row + 16 : row + 32, start * OBS : start * OBS + source.shape[1]] = lo

    renew(32, zf[16:32, :], W)

    def upper(b):
        zf[32:48, lanes(b - W)] = 0.5 * obs_v[pl.ds(b - W, 1), :] * zf[16:32, lanes(b - W)]
        gather(b, 0, HALF, 32)

    def uppers(i, carry):
        for more in range(UNROLL):
            upper(W + i * UNROLL + more)
        return carry

    lax.fori_loop(0, (last - W) // UNROLL, uppers, 0)
    for b in range(last, last + W):
        upper_lanes = lanes(b - W)
        zf[32:48, upper_lanes] = 0.5 * obs_v[b - W : b - W + 1, :] * zf[16:32, upper_lanes]
        gather(b, 0, last + W - b, 32)
    lane = lax.broadcasted_iota(jnp.int32, (16, OBS), 1)
    lane8 = lax.broadcasted_iota(jnp.int32, (8, OBS), 1)

    def turn(value, by):
        return pltpu.roll(value, by % OBS, 1)

    def product_gram(left_rows, right_rows):
        value = lax.dot_general(left_rows, right_rows, (((1,), (1,)), ((), ())), preferred_element_type=F32)
        height, width = value.shape
        value = jnp.concatenate([value, jnp.zeros((height, OBS - width), F32)], axis=1)
        value = value[0:16] + value[16:32] if height == 32 else value
        return value + turn(value, -16) if height == 32 else value

    own = slice(W * OBS, (W + NB) * OBS)
    renew(64, zf[32:48, :], W)
    of_r = product_gram(zx[0:32, own], zx[0:64, own])
    of_p = product_gram(zx[32:64, own], zx[32:96, own])
    of_h = product_gram(zx[64:96, own], zx[32:64, own])
    place = lane >> 4
    early = jnp.where(
        place == 0, of_r, jnp.where(place == 1, turn(of_p, 16), jnp.where(place == 2, of_r, turn(of_p, 16) + turn(of_h, 48)))
    )
    across = [None] * W
    for b in range(last, last + W):
        start = last + W - b
        vectors = zx[32:64, b * OBS : (b + 1) * OBS]
        part = lax.dot_general(
            jnp.concatenate([vectors, vectors], axis=1), kmat[b, start * OBS :, :],
            (((1,), (1,)), ((), ())), preferred_element_type=F32,
        )
        part = (part[0:16] + part[16:32]) * STATIC_VAR
        for i in range(HALF - start):
            piece = part[:, i * OBS : (i + 1) * OBS]
            across[i] = piece if across[i] is None else across[i] + piece
    across = jnp.concatenate(split(jnp.concatenate(across, axis=1)), axis=0)
    to_left.wait()
    theirs = jnp.concatenate(split(p_hi[...]), axis=0)
    late = product_gram(across, theirs) + product_gram(theirs, across)
    own_part = jnp.where(place == 3, early + turn(late, 48), early)
    part_a[...] = jnp.where(lane8 < 64, own_part[0:8], turn(own_part[8:16], 64))

    def exchange(part, red, peers, send, recv):
        copies = [
            pltpu.make_async_remote_copy(
                src_ref=part, dst_ref=red.at[i], send_sem=send.at[i], recv_sem=recv.at[i],
                device_id=there, device_id_type=MESH,
            )
            for i, there in enumerate(peers)
        ]
        for copy in copies:
            copy.start()
        return copies

    first_sum = exchange(part_a, red_a, peers_a, send_a, recv_a)

    def rest(i, carry):
        for more in range(UNROLL):
            scatter(W + i * UNROLL + more, 0, HALF, 32)
        return carry

    renew(32, p_hi[...], NB + W)
    for b in range(last, last + W):
        gather(b, last + W - b, HALF, 32)
    to_right.wait()
    renew(32, p_lo[...], 0)
    for b in range(W):
        scatter(b, W - b, HALF, 32)
    lax.fori_loop(0, (last - W) // UNROLL, rest, 0)
    for b in range(last, last + W):
        scatter(b, 0, last + W - b, 32)

    def other_half(i, carry):
        zf[32:48, lanes(i)] += 0.5 * obs_v[pl.ds(i, 1), :] * zf[16:32, lanes(i)]
        return carry

    lax.fori_loop(0, NB, other_half, 0)
    for copy in first_sum:
        copy.wait_recv()
    part_b[...] = part_a[...] + jnp.sum(red_a[...], axis=0)
    second_sum = exchange(part_b, red_b, peers_b, send_b, recv_b)
    for copy in first_sum:
        copy.wait_send()
    for copy in second_sum:
        copy.wait_recv()
    packed = part_b[...] + jnp.sum(red_b[...], axis=0)

    moments = jnp.concatenate([packed, turn(packed, 64)], axis=0)
    rows = lax.broadcasted_iota(jnp.int32, (32, OBS), 0)

    def column(at):
        return jnp.broadcast_to(moments[:, at : at + 1], (16, OBS))

    system = jnp.concatenate([moments, turn(moments, -32)], axis=0)
    middle = [column(16 + j) for j in range(16)]
    spread = [jnp.concatenate([column(32 + j), middle[j]], axis=0) for j in range(16)]
    spread += [jnp.concatenate([middle[j], column(48 + j)], axis=0) for j in range(16)]
    inverses = []
    for k in range(32):
        inverse = 1.0 / spread[k][k : k + 1, :]
        factor = jnp.where(rows == k, 0.0, spread[k] * inverse)
        for j in range(k + 1, 32):
            spread[j] = spread[j] - factor * spread[j][k : k + 1, :]
        system = system - factor * system[k : k + 1, :]
        inverses.append(inverse)
    system = system * jnp.concatenate(inverses, axis=0)

    solved = jnp.concatenate([system, jnp.zeros((96, OBS), F32)], axis=0).T
    for_w = jnp.where(lane < 32, solved[0:16, :], 0.0)
    both = jnp.concatenate([for_w, turn(for_w, 16)], axis=0)[:, 0:48]
    for chunk in range(4):
        here = slice(chunk * 4 * OBS, (chunk + 1) * 4 * OBS)
        sums = jnp.dot(both, zf[:, here], preferred_element_type=F32, precision=lax.Precision.HIGHEST)
        left_over = zf[0:16, here] - sums[16:32]
        for piece in range(4):
            b = chunk * 4 + piece
            w_out[b] = sums[0:16, piece * OBS : (piece + 1) * OBS]
            r_out[b] = left_over[:, piece * OBS : (piece + 1) * OBS]
    for copy in second_sum:
        copy.wait_send()


def on_device(innovations, ensemble, coords, obs_error, pair_cols, pair_count):
    del pair_count
    vmem = pl.BlockSpec(memory_space=pltpu.VMEM)
    arrays = [pltpu.with_memory_space_constraint(a, pltpu.HBM) for a in (innovations, ensemble, coords, obs_error, pair_cols)]
    out = jax.ShapeDtypeStruct((NB, RHS, OBS), F32)
    return pl.pallas_call(
        kernel,
        out_shape=(out, out),
        in_specs=[pl.BlockSpec(memory_space=pltpu.HBM)] * 5,
        out_specs=(vmem, vmem),
        scratch_shapes=[
            pltpu.VMEM((NB, MEM, OBS), F32),
            pltpu.VMEM((NB, 2, OBS), jnp.int32),
            pltpu.VMEM((NB, RHS, OBS), F32),
            pltpu.VMEM((NB, OBS), F32),
            pltpu.VMEM((NB, SLOTS), jnp.int32),
            pltpu.VMEM(((NB + W) * OBS, 256), BF16),
            pltpu.VMEM((NB + W, 256, 256), BF16),
            pltpu.VMEM((NB + W, HALF * OBS, 256), BF16),
            pltpu.VMEM((96, NX * OBS), BF16),
            pltpu.VMEM((48, NB * OBS), F32),
            pltpu.VMEM((SLOTS, NB, OBS), F32),
            pltpu.VMEM((W, MEM, OBS), F32),
            pltpu.VMEM((W, MEM, OBS), F32),
            pltpu.VMEM((W, 2, OBS), jnp.int32),
            pltpu.VMEM((W, 2, OBS), jnp.int32),
            pltpu.VMEM((W, RHS, OBS), F32),
            pltpu.VMEM((W, RHS, OBS), F32),
            pltpu.VMEM((RHS, W * OBS), F32),
            pltpu.VMEM((RHS, W * OBS), F32),
            pltpu.VMEM((8, OBS), F32),
            pltpu.VMEM((8, OBS), F32),
            pltpu.VMEM((15, 8, OBS), F32),
            pltpu.VMEM((15, 8, OBS), F32),
            pltpu.SemaphoreType.DMA((5,)),
            pltpu.SemaphoreType.DMA((14,)),
            pltpu.SemaphoreType.DMA((14,)),
            pltpu.SemaphoreType.DMA((15,)),
            pltpu.SemaphoreType.DMA((15,)),
            pltpu.SemaphoreType.DMA((15,)),
            pltpu.SemaphoreType.DMA((15,)),
        ],
        compiler_params=pltpu.CompilerParams(
            collective_id=0, has_side_effects=True, vmem_limit_bytes=LIMIT
        ),
    )(*arrays)


def solution(mesh):
    both = ("region", "sub")
    in_specs = (
        P(both, None, None),
        P(both, None, None),
        P(both, None, None),
        P(both, None),
        P(both, None),
        P(both),
    )
    out_specs = (P(both, None, None), P(both, None, None))
    return jax.shard_map(on_device, mesh=mesh, in_specs=in_specs, out_specs=out_specs, check_vma=False)
```

```python
import jax
import jax.numpy as jnp
from jax import lax
from jax.experimental import pallas as pl
from jax.experimental.pallas import tpu as pltpu
from jax.sharding import PartitionSpec as P

MESH = pl.DeviceIdType.MESH
F32 = jnp.float32
BF16 = jnp.bfloat16

LIMIT = 40 * 1024 * 1024
UNROLL = 4
EARLY = 3
NB = 16
W = 4
NX = NB + 2 * W
SLOTS = 2 * W + 1
HALF = W + 1
OBS = 128
RHS = 16
MEM = 64

STATIC_VAR = 0.002
LOG2E = 1.4426950408889634
C_CORR = -LOG2E / 150.0
C_LOC = -LOG2E / (2.0 * 200.0**2)
ENS_SCALE = 1.0 / ((MEM - 1) * STATIC_VAR)


def split(value):
    hi = value.astype(BF16)
    lo = (value - hi.astype(F32)).astype(BF16)
    return hi, lo


def half_first(value):
    first = value[:, 0:OBS] * 0.5
    return first if value.shape[1] == OBS else jnp.concatenate([first, value[:, OBS:]], axis=1)


def rows_of(rows):
    ids = lax.broadcasted_iota(jnp.int32, (16, OBS), 0)
    out = jnp.zeros((16, OBS), F32)
    for place, row in enumerate(rows):
        out = jnp.where(ids == place, jnp.broadcast_to(row, (16, OBS)), out)
    return out.astype(BF16)


def position_parts(crd, place):
    x = crd[0:1, :].astype(F32)
    y = crd[1:2, :].astype(F32)
    base = jnp.full((1, OBS), jnp.asarray(place - NX // 2).astype(F32) * 64.0, F32)
    full = x + base
    square = full * full + y * y
    s1 = square.astype(BF16).astype(F32)
    s2 = (square - s1).astype(BF16).astype(F32)
    s3 = square - s1 - s2
    return s1, s2, s3, base, x, y


def kernel(
    innov, ens, coords, obs, cols, w_out, r_out,
    ens_v, crd_v, v_v, obs_v, cols_v,
    lhsx, rhs, kmat, zx, zf, maskx,
    ens_lo, ens_hi, crd_lo, crd_hi, v_lo, v_hi, p_lo, p_hi, edge_lo, edge_hi,
    part_a, part_b, red_a, red_b,
    load_sem, halo_send, halo_recv, send_a, recv_a, send_b, recv_b,
):
    me = lax.axis_index("region") * 4 + lax.axis_index("sub")

    def device(index):
        return (lax.div(index, 4), lax.rem(index, 4))

    left = device(lax.rem(me + 255, 256))
    right = device(lax.rem(me + 1, 256))
    x = lax.rem(me, 4)
    core = lax.rem(lax.div(me, 4), 2)
    y = lax.rem(lax.div(me, 8), 4)
    z = lax.div(me, 32)

    def peer_a(dy, dx):
        return device(((z * 4 + lax.rem(y + dy, 4)) * 2 + core) * 4 + lax.rem(x + dx, 4))

    def peer_b(dz, dc):
        return device(((lax.rem(z + dz, 8) * 4 + y) * 2 + lax.rem(core + dc, 2)) * 4 + x)

    peers_a = [peer_a(dy, dx) for dy, dx in sorted(
        ((dy, dx) for dy in range(4) for dx in range(4) if dy or dx),
        key=lambda by: -min(by[0], 4 - by[0]) - min(by[1], 4 - by[1]),
    )]
    peers_b = [peer_b(dz, dc) for dz, dc in sorted(
        ((dz, dc) for dz in range(8) for dc in range(2) if dz or dc),
        key=lambda by: -2 * min(by[0], 8 - by[0]) - by[1],
    )]

    loads = [
        pltpu.make_async_copy(source, target, load_sem.at[i])
        for i, (source, target) in enumerate(
            ((cols, cols_v), (coords, crd_v), (ens, ens_v), (innov, v_v), (obs, obs_v))
        )
    ]
    for load in loads:
        load.start()
    barrier = pltpu.get_barrier_semaphore()
    for there in (left, right):
        pl.semaphore_signal(barrier, inc=1, device_id=there, device_id_type=MESH)

    for there in peers_b + peers_a:
        pl.semaphore_signal(barrier, inc=1, device_id=there, device_id_type=MESH)
    pl.semaphore_wait(barrier, 32)

    def remote(src, dst, slot, there):
        return pltpu.make_async_remote_copy(
            src_ref=src, dst_ref=dst, send_sem=halo_send.at[slot], recv_sem=halo_recv.at[slot],
            device_id=there, device_id_type=MESH,
        )

    small = [
        remote(coords.at[NB - W : NB], crd_lo, 0, right),
        remote(coords.at[0:W], crd_hi, 1, left),
        remote(innov.at[NB - W : NB], v_lo, 2, right),
        remote(innov.at[0:W], v_hi, 3, left),
    ]
    blocks = [
        (
            remote(ens.at[NB - 1 - q], ens_lo.at[W - 1 - q], 4 + 2 * q, right),
            remote(ens.at[q], ens_hi.at[q], 5 + 2 * q, left),
        )
        for q in range(W)
    ]
    for copy in small:
        copy.start()
    for pair in blocks:
        for copy in pair:
            copy.start()
    for load in loads:
        load.wait()

    offset = cols_v[...] - (lax.broadcasted_iota(jnp.int32, (NB, SLOTS), 0) + me * NB)
    for slot in range(SLOTS):
        hit = jnp.max(jnp.where(offset == slot - W, 1.0, 0.0).astype(F32), axis=1, keepdims=True)
        maskx[slot] = jnp.broadcast_to(hit, (NB, OBS))

    def lanes(place, count=1):
        return pl.ds(pl.multiple_of(place * OBS, OBS), count * OBS)

    def set_vectors(place, vectors):
        hi, lo = split(vectors)
        zx[0:16, lanes(place)] = hi
        zx[16:32, lanes(place)] = lo

    def set_left(place, members, crd):
        hi, lo = split(members)
        s1, s2, s3, base, x, y = position_parts(crd, place)
        one = jnp.ones((1, OBS), F32)
        parts = rows_of([s1, s2, s3, one, one, one, base, base, x, x, y])
        stacked = jnp.concatenate([hi, hi, lo, parts, jnp.zeros((48, OBS), BF16)], axis=0)
        lhsx[pl.ds(pl.multiple_of((place - W) * OBS, OBS), OBS), :] = stacked.T

    def set_right(place, members, crd):
        hi, lo = split(members * ENS_SCALE)
        s1, s2, s3, base, x, y = position_parts(crd, place)
        one = jnp.ones((1, OBS), F32)
        parts = rows_of([one, one, one, s1, s2, s3, -2.0 * base, -2.0 * x, -2.0 * base, -2.0 * x, -2.0 * y])
        rhs[place, 0:64, 0:128] = hi
        rhs[place, 64:128, 0:128] = lo
        rhs[place, 128:192, 0:128] = hi
        rhs[place, 192:256, 0:128] = jnp.zeros((64, OBS), BF16)
        rhs[place, 0:192, 128:256] = jnp.zeros((192, OBS), BF16)
        rhs[place, 192:208, 128:256] = parts
        rhs[place, 208:256, 128:256] = jnp.zeros((48, OBS), BF16)

    def prepare_own(i, carry):
        members = ens_v[i]
        vectors = v_v[i]
        set_left(i + W, members, crd_v[i])
        set_right(i + W, members, crd_v[i])
        set_vectors(i + W, vectors)
        zf[0:16, lanes(i)] = vectors
        zf[16:32, lanes(i)] = obs_v[pl.ds(i, 1), :] * vectors
        return carry

    lax.fori_loop(0, NB, prepare_own, 0)

    def tiles(b, start, stop, mask):
        count = stop - start
        here = pl.ds(pl.multiple_of((b + start - W) * OBS, OBS), count * OBS)
        every = jnp.dot(lhsx[here, :], rhs[b], preferred_element_type=F32)
        for j in range(start, stop):
            both = every[(j - start) * OBS : (j - start + 1) * OBS]
            shared = both[:, 0:128]
            square = both[:, 128:256]
            inverse = lax.rsqrt(jnp.maximum(square, 1e-30))
            value = jnp.exp2(square * C_CORR * inverse) + jnp.exp2(square * C_LOC) * shared
            hi, lo = split(value * mask(b, j))
            kmat[b, j * OBS : (j + 1) * OBS, 0:128] = hi
            kmat[b, j * OBS : (j + 1) * OBS, 128:256] = lo

    def own_mask(b, j):
        return maskx[j + W, pl.ds(b - W, 1), :]

    def low_mask(b, j):
        return maskx[W - j, b + j - W : b + j - W + 1, :]

    def add(row, place, count, part):
        part = part[0:16] + part[16:32]
        zf[row : row + 16, lanes(place - W, count)] += part * STATIC_VAR

    def gather(b, start, stop, row):
        vectors = zx[row : row + 32, lanes(b + start, stop - start)]
        if row and start == 0:
            vectors = half_first(vectors)
        part = jnp.dot(
            vectors, kmat[b, start * OBS : stop * OBS, :],
            preferred_element_type=F32,
        )
        add(row // 2 + 16, b, 1, part[:, 0:128] + part[:, 128:256])

    def scatter(b, start, stop, row):
        vectors = zx[row : row + 32, lanes(b)]
        part = lax.dot_general(
            jnp.concatenate([vectors, vectors], axis=1), kmat[b, start * OBS : stop * OBS, :],
            (((1,), (1,)), ((), ())), preferred_element_type=F32,
        )
        if row and start == 0:
            part = half_first(part)
        add(row // 2 + 16, b + start, stop - start, part)

    last = NB

    def apply_to(b, inside):
        gather(b, 0, inside, 0)
        if inside > 1:
            scatter(b, 1, inside, 0)

    def step(b, carry):
        apply_to(b - 1, HALF)
        tiles(b, 0, HALF, own_mask)
        return carry

    tiles(W, 0, HALF, own_mask)
    lax.fori_loop(W + 1, 2 * W + 1, step, 0)
    edge_lo[...] = zf[16:32, 0 : W * OBS]
    to_left = remote(edge_lo, p_hi, 12, left)
    to_left.start()
    lax.fori_loop(2 * W + 1, 2 * W + EARLY, step, 0)
    tiles(last - W, W, HALF, own_mask)
    apply_to(2 * W + EARLY - 1, HALF)
    for b in range(last - W + 1, last):
        tiles(b, last - b, HALF, own_mask)
        scatter(b - 1, last + 1 - b, HALF, 0)
    tiles(last, 0, W, own_mask)
    scatter(last - 1, 1, HALF, 0)
    for b in range(last + 1, last + W):
        tiles(b, 0, last + W - b, own_mask)
        apply_to(b - 1, last + W + 1 - b)
    apply_to(last + W - 1, 1)

    edge_hi[...] = zf[16:32, (NB - W) * OBS : NB * OBS]
    to_right = remote(edge_hi, p_lo, 13, right)
    to_right.start()

    small[0].wait()
    small[2].wait()
    for q in range(W):
        set_vectors(q, v_lo[q])
    for q in range(W):
        low = W - 1 - q
        blocks[q][0].wait()
        set_right(low, ens_lo[low], crd_lo[low])
        tiles(low, q + 1, HALF, low_mask)
        if q:
            scatter(low + 1, q, HALF, 0)
    scatter(0, W, HALF, 0)

    small[1].wait()
    small[3].wait()
    for q in range(W):
        set_vectors(q + NB + W, v_hi[q])
    for q in range(W):
        high = last + W + q
        blocks[q][1].wait()
        set_left(high, ens_hi[q], crd_hi[q])
        for j in range(q + 1, HALF):
            tiles(high - j, j, j + 1, own_mask)
    for b in range(last, last + W):
        gather(b, last + W - b, HALF, 0)

    tiles(2 * W + EARLY, 0, HALF, own_mask)
    lax.fori_loop(2 * W + EARLY + 1, last - W, step, 0)
    tiles(last - W, 0, W, own_mask)
    apply_to(last - W - 1, HALF)
    for b in range(last - W + 1, last):
        tiles(b, 0, last - b, own_mask)
        gather(b - 1, 0, HALF, 0)
        scatter(b - 1, 1, last + 1 - b, 0)
    gather(last - 1, 0, HALF, 0)

    def renew(row, source, start):
        hi, lo = split(source)
        zx[row : row + 16, start * OBS : start * OBS + source.shape[1]] = hi
        zx[row + 16 : row + 32, start * OBS : start * OBS + source.shape[1]] = lo

    renew(32, zf[16:32, :], W)

    def upper(b):
        zf[32:48, lanes(b - W)] = 0.5 * obs_v[pl.ds(b - W, 1), :] * zf[16:32, lanes(b - W)]
        gather(b, 0, HALF, 32)

    def uppers(i, carry):
        for more in range(UNROLL):
            upper(W + i * UNROLL + more)
        return carry

    lax.fori_loop(0, (last - W) // UNROLL, uppers, 0)
    for b in range(last, last + W):
        upper_lanes = lanes(b - W)
        zf[32:48, upper_lanes] = 0.5 * obs_v[b - W : b - W + 1, :] * zf[16:32, upper_lanes]
        gather(b, 0, last + W - b, 32)
    lane = lax.broadcasted_iota(jnp.int32, (16, OBS), 1)
    lane8 = lax.broadcasted_iota(jnp.int32, (8, OBS), 1)

    def turn(value, by):
        return pltpu.roll(value, by % OBS, 1)

    def product_gram(left_rows, right_rows):
        value = lax.dot_general(left_rows, right_rows, (((1,), (1,)), ((), ())), preferred_element_type=F32)
        height, width = value.shape
        value = jnp.concatenate([value, jnp.zeros((height, OBS - width), F32)], axis=1)
        value = value[0:16] + value[16:32] if height == 32 else value
        return value + turn(value, -16) if height == 32 else value

    own = slice(W * OBS, (W + NB) * OBS)
    renew(64, zf[32:48, :], W)
    of_r = product_gram(zx[0:32, own], zx[0:64, own])
    of_p = product_gram(zx[32:64, own], zx[32:96, own])
    of_h = product_gram(zx[64:96, own], zx[32:64, own])
    place = lane >> 4
    early = jnp.where(
        place == 0, of_r, jnp.where(place == 1, turn(of_p, 16), jnp.where(place == 2, of_r, turn(of_p, 16) + turn(of_h, 48)))
    )
    def across(row):
        sums = [None] * W
        for b in range(last, last + W):
            start = last + W - b
            vectors = zx[row : row + 32, b * OBS : (b + 1) * OBS]
            part = lax.dot_general(
                jnp.concatenate([vectors, vectors], axis=1), kmat[b, start * OBS :, :],
                (((1,), (1,)), ((), ())), preferred_element_type=F32,
            )
            part = (part[0:16] + part[16:32]) * STATIC_VAR
            for i in range(HALF - start):
                piece = part[:, i * OBS : (i + 1) * OBS]
                sums[i] = piece if sums[i] is None else sums[i] + piece
        return jnp.concatenate(sums, axis=1)

    ours = jnp.concatenate(split(across(32)), axis=0)
    given = across(0)
    to_left.wait()
    upper_halo = p_hi[...] + given
    theirs = jnp.concatenate(split(upper_halo), axis=0)
    late = product_gram(ours, theirs) + product_gram(theirs, ours)
    own_part = jnp.where(place == 3, early + turn(late, 48), early)
    part_a[...] = jnp.where(lane8 < 64, own_part[0:8], turn(own_part[8:16], 64))

    def exchange(part, red, peers, send, recv):
        copies = [
            pltpu.make_async_remote_copy(
                src_ref=part, dst_ref=red.at[i], send_sem=send.at[i], recv_sem=recv.at[i],
                device_id=there, device_id_type=MESH,
            )
            for i, there in enumerate(peers)
        ]
        for copy in copies:
            copy.start()
        return copies

    first_sum = exchange(part_a, red_a, peers_a, send_a, recv_a)

    def rest(i, carry):
        for more in range(UNROLL):
            scatter(W + i * UNROLL + more, 0, HALF, 32)
        return carry

    renew(32, upper_halo, NB + W)
    for b in range(last, last + W):
        gather(b, last + W - b, HALF, 32)
    to_right.wait()
    lower_halo = []
    for b in range(W):
        part = jnp.dot(
            zx[0:32, W * OBS : (b + HALF) * OBS], kmat[b, (W - b) * OBS :, :], preferred_element_type=F32
        )
        part = part[0:16] + part[16:32]
        part = (part[:, 0:128] + part[:, 128:256]) * STATIC_VAR
        lower_halo.append(p_lo[:, b * OBS : (b + 1) * OBS] + part)
    renew(32, jnp.concatenate(lower_halo, axis=1), 0)
    for b in range(W):
        scatter(b, W - b, HALF, 32)
    lax.fori_loop(0, (last - W) // UNROLL, rest, 0)
    for b in range(last, last + W):
        scatter(b, 0, last + W - b, 32)

    def other_half(i, carry):
        zf[32:48, lanes(i)] += 0.5 * obs_v[pl.ds(i, 1), :] * zf[16:32, lanes(i)]
        return carry

    lax.fori_loop(0, NB, other_half, 0)
    for copy in first_sum:
        copy.wait_recv()
    part_b[...] = part_a[...] + jnp.sum(red_a[...], axis=0)
    second_sum = exchange(part_b, red_b, peers_b, send_b, recv_b)
    for copy in first_sum:
        copy.wait_send()
    for copy in second_sum:
        copy.wait_recv()
    packed = part_b[...] + jnp.sum(red_b[...], axis=0)

    moments = jnp.concatenate([packed, turn(packed, 64)], axis=0)
    rows = lax.broadcasted_iota(jnp.int32, (32, OBS), 0)

    lower = turn(moments, -32)
    system = jnp.concatenate([moments, lower], axis=0)
    first_half = [
        jnp.concatenate(
            [
                jnp.broadcast_to(moments[:, 32 + j : 33 + j], (16, OBS)),
                jnp.broadcast_to(moments[:, 16 + j : 17 + j], (16, OBS)),
            ],
            axis=0,
        )
        for j in range(16)
    ]

    def eliminate(spread, system, base):
        inverses = []
        for i in range(16):
            k = base + i
            inverse = 1.0 / spread[i][k : k + 1, :]
            factor = jnp.where(rows == k, 0.0, spread[i] * inverse)
            for j in range(i + 1, 16):
                spread[j] = spread[j] - factor * spread[j][k : k + 1, :]
            system = system - factor * system[k : k + 1, :]
            inverses.append(inverse)
        scaled = system[base : base + 16] * jnp.concatenate(inverses, axis=0)
        return jnp.concatenate([system[0:16], scaled] if base else [scaled, system[16:32]], axis=0)

    system = eliminate(first_half, system, 0)
    second_half = [jnp.broadcast_to(system[:, 16 + j : 17 + j], (32, OBS)) for j in range(16)]
    system = eliminate(second_half, system, 16)

    solved = jnp.concatenate([system, jnp.zeros((96, OBS), F32)], axis=0).T
    for_w = jnp.where(lane < 32, solved[0:16, :], 0.0)
    both = jnp.concatenate([for_w, turn(for_w, 16)], axis=0)[:, 0:48]
    for chunk in range(4):
        here = slice(chunk * 4 * OBS, (chunk + 1) * 4 * OBS)
        sums = jnp.dot(both, zf[:, here], preferred_element_type=F32, precision=lax.Precision.HIGHEST)
        left_over = zf[0:16, here] - sums[16:32]
        for piece in range(4):
            b = chunk * 4 + piece
            w_out[b] = sums[0:16, piece * OBS : (piece + 1) * OBS]
            r_out[b] = left_over[:, piece * OBS : (piece + 1) * OBS]
    for copy in second_sum:
        copy.wait_send()


def on_device(innovations, ensemble, coords, obs_error, pair_cols, pair_count):
    del pair_count
    vmem = pl.BlockSpec(memory_space=pltpu.VMEM)
    arrays = [pltpu.with_memory_space_constraint(a, pltpu.HBM) for a in (innovations, ensemble, coords, obs_error, pair_cols)]
    out = jax.ShapeDtypeStruct((NB, RHS, OBS), F32)
    return pl.pallas_call(
        kernel,
        out_shape=(out, out),
        in_specs=[pl.BlockSpec(memory_space=pltpu.HBM)] * 5,
        out_specs=(vmem, vmem),
        scratch_shapes=[
            pltpu.VMEM((NB, MEM, OBS), F32),
            pltpu.VMEM((NB, 2, OBS), jnp.int32),
            pltpu.VMEM((NB, RHS, OBS), F32),
            pltpu.VMEM((NB, OBS), F32),
            pltpu.VMEM((NB, SLOTS), jnp.int32),
            pltpu.VMEM(((NB + W) * OBS, 256), BF16),
            pltpu.VMEM((NB + W, 256, 256), BF16),
            pltpu.VMEM((NB + W, HALF * OBS, 256), BF16),
            pltpu.VMEM((96, NX * OBS), BF16),
            pltpu.VMEM((48, NB * OBS), F32),
            pltpu.VMEM((SLOTS, NB, OBS), F32),
            pltpu.VMEM((W, MEM, OBS), F32),
            pltpu.VMEM((W, MEM, OBS), F32),
            pltpu.VMEM((W, 2, OBS), jnp.int32),
            pltpu.VMEM((W, 2, OBS), jnp.int32),
            pltpu.VMEM((W, RHS, OBS), F32),
            pltpu.VMEM((W, RHS, OBS), F32),
            pltpu.VMEM((RHS, W * OBS), F32),
            pltpu.VMEM((RHS, W * OBS), F32),
            pltpu.VMEM((RHS, W * OBS), F32),
            pltpu.VMEM((RHS, W * OBS), F32),
            pltpu.VMEM((8, OBS), F32),
            pltpu.VMEM((8, OBS), F32),
            pltpu.VMEM((15, 8, OBS), F32),
            pltpu.VMEM((15, 8, OBS), F32),
            pltpu.SemaphoreType.DMA((5,)),
            pltpu.SemaphoreType.DMA((14,)),
            pltpu.SemaphoreType.DMA((14,)),
            pltpu.SemaphoreType.DMA((15,)),
            pltpu.SemaphoreType.DMA((15,)),
            pltpu.SemaphoreType.DMA((15,)),
            pltpu.SemaphoreType.DMA((15,)),
        ],
        compiler_params=pltpu.CompilerParams(
            collective_id=0, has_side_effects=True, vmem_limit_bytes=LIMIT
        ),
    )(*arrays)


def solution(mesh):
    both = ("region", "sub")
    in_specs = (
        P(both, None, None),
        P(both, None, None),
        P(both, None, None),
        P(both, None),
        P(both, None),
        P(both),
    )
    out_specs = (P(both, None, None), P(both, None, None))
    return jax.shard_map(on_device, mesh=mesh, in_specs=in_specs, out_specs=out_specs, check_vma=False)
```

```python
import jax
import jax.numpy as jnp
from jax import lax
from jax.experimental import pallas as pl
from jax.experimental.pallas import tpu as pltpu
from jax.sharding import PartitionSpec as P

MESH = pl.DeviceIdType.MESH
F32 = jnp.float32
BF16 = jnp.bfloat16

LIMIT = 40 * 1024 * 1024
UNROLL = 6
EARLY = 3
NB = 16
W = 4
NX = NB + 2 * W
SLOTS = 2 * W + 1
HALF = W + 1
OBS = 128
RHS = 16
MEM = 64

STATIC_VAR = 0.002
LOG2E = 1.4426950408889634
C_CORR = -LOG2E / 150.0
C_LOC = -LOG2E / (2.0 * 200.0**2)
ENS_SCALE = 1.0 / ((MEM - 1) * STATIC_VAR)


def split(value):
    hi = value.astype(BF16)
    lo = (value - hi.astype(F32)).astype(BF16)
    return hi, lo


def half_first(value):
    first = value[:, 0:OBS] * 0.5
    return first if value.shape[1] == OBS else jnp.concatenate([first, value[:, OBS:]], axis=1)


def rows_of(rows):
    ids = lax.broadcasted_iota(jnp.int32, (16, OBS), 0)
    out = jnp.zeros((16, OBS), F32)
    for place, row in enumerate(rows):
        out = jnp.where(ids == place, jnp.broadcast_to(row, (16, OBS)), out)
    return out.astype(BF16)


def position_parts(crd, place):
    x = crd[0:1, :].astype(F32)
    y = crd[1:2, :].astype(F32)
    base = jnp.full((1, OBS), jnp.asarray(place - NX // 2).astype(F32) * 64.0, F32)
    full = x + base
    square = full * full + y * y
    s1 = square.astype(BF16).astype(F32)
    s2 = (square - s1).astype(BF16).astype(F32)
    s3 = square - s1 - s2
    return s1, s2, s3, base, x, y


def kernel(
    innov, ens, coords, obs, cols, w_out, r_out,
    ens_v, crd_v, v_v, obs_v, cols_v,
    lhsx, rhs, kmat, zx, zf, maskx,
    ens_lo, ens_hi, crd_lo, crd_hi, v_lo, v_hi, p_lo, p_hi, edge_lo, edge_hi,
    part_a, part_b, red_a, red_b,
    load_sem, halo_send, halo_recv, send_a, recv_a, send_b, recv_b,
):
    me = lax.axis_index("region") * 4 + lax.axis_index("sub")

    def device(index):
        return (lax.div(index, 4), lax.rem(index, 4))

    left = device(lax.rem(me + 255, 256))
    right = device(lax.rem(me + 1, 256))
    x = lax.rem(me, 4)
    core = lax.rem(lax.div(me, 4), 2)
    y = lax.rem(lax.div(me, 8), 4)
    z = lax.div(me, 32)

    def peer_a(dy, dx):
        return device(((z * 4 + lax.rem(y + dy, 4)) * 2 + core) * 4 + lax.rem(x + dx, 4))

    def peer_b(dz, dc):
        return device(((lax.rem(z + dz, 8) * 4 + y) * 2 + lax.rem(core + dc, 2)) * 4 + x)

    peers_a = [peer_a(dy, dx) for dy, dx in sorted(
        ((dy, dx) for dy in range(4) for dx in range(4) if dy or dx),
        key=lambda by: -min(by[0], 4 - by[0]) - min(by[1], 4 - by[1]),
    )]
    peers_b = [peer_b(dz, dc) for dz, dc in sorted(
        ((dz, dc) for dz in range(8) for dc in range(2) if dz or dc),
        key=lambda by: -2 * min(by[0], 8 - by[0]) - by[1],
    )]

    loads = [
        pltpu.make_async_copy(source, target, load_sem.at[i])
        for i, (source, target) in enumerate(
            ((cols, cols_v), (coords, crd_v), (ens, ens_v), (innov, v_v), (obs, obs_v))
        )
    ]
    for load in loads:
        load.start()
    barrier = pltpu.get_barrier_semaphore()
    for there in (left, right):
        pl.semaphore_signal(barrier, inc=1, device_id=there, device_id_type=MESH)

    for there in peers_b + peers_a:
        pl.semaphore_signal(barrier, inc=1, device_id=there, device_id_type=MESH)
    pl.semaphore_wait(barrier, 32)

    def remote(src, dst, slot, there):
        return pltpu.make_async_remote_copy(
            src_ref=src, dst_ref=dst, send_sem=halo_send.at[slot], recv_sem=halo_recv.at[slot],
            device_id=there, device_id_type=MESH,
        )

    small = [
        remote(coords.at[NB - W : NB], crd_lo, 0, right),
        remote(coords.at[0:W], crd_hi, 1, left),
        remote(innov.at[NB - W : NB], v_lo, 2, right),
        remote(innov.at[0:W], v_hi, 3, left),
    ]
    blocks = [
        (
            remote(ens.at[NB - 1 - q], ens_lo.at[W - 1 - q], 4 + 2 * q, right),
            remote(ens.at[q], ens_hi.at[q], 5 + 2 * q, left),
        )
        for q in range(W)
    ]
    for copy in small:
        copy.start()
    for pair in blocks:
        for copy in pair:
            copy.start()
    for load in loads:
        load.wait()

    offset = cols_v[...] - (lax.broadcasted_iota(jnp.int32, (NB, SLOTS), 0) + me * NB)
    for slot in range(SLOTS):
        hit = jnp.max(jnp.where(offset == slot - W, 1.0, 0.0).astype(F32), axis=1, keepdims=True)
        maskx[slot] = jnp.broadcast_to(hit, (NB, OBS))

    def lanes(place, count=1):
        return pl.ds(pl.multiple_of(place * OBS, OBS), count * OBS)

    def set_vectors(place, vectors):
        hi, lo = split(vectors)
        zx[0:16, lanes(place)] = hi
        zx[16:32, lanes(place)] = lo

    def set_left(place, members, crd):
        hi, lo = split(members)
        s1, s2, s3, base, x, y = position_parts(crd, place)
        one = jnp.ones((1, OBS), F32)
        parts = rows_of([s1, s2, s3, one, one, one, base, base, x, x, y])
        stacked = jnp.concatenate([hi, hi, lo, parts, jnp.zeros((48, OBS), BF16)], axis=0)
        lhsx[pl.ds(pl.multiple_of((place - W) * OBS, OBS), OBS), :] = stacked.T

    def set_right(place, members, crd):
        hi, lo = split(members * ENS_SCALE)
        s1, s2, s3, base, x, y = position_parts(crd, place)
        one = jnp.ones((1, OBS), F32)
        parts = rows_of([one, one, one, s1, s2, s3, -2.0 * base, -2.0 * x, -2.0 * base, -2.0 * x, -2.0 * y])
        rhs[place, 0:64, 0:128] = hi
        rhs[place, 64:128, 0:128] = lo
        rhs[place, 128:192, 0:128] = hi
        rhs[place, 192:256, 0:128] = jnp.zeros((64, OBS), BF16)
        rhs[place, 0:192, 128:256] = jnp.zeros((192, OBS), BF16)
        rhs[place, 192:208, 128:256] = parts
        rhs[place, 208:256, 128:256] = jnp.zeros((48, OBS), BF16)

    def prepare_own(i, carry):
        members = ens_v[i]
        vectors = v_v[i]
        set_left(i + W, members, crd_v[i])
        set_right(i + W, members, crd_v[i])
        set_vectors(i + W, vectors)
        zf[0:16, lanes(i)] = vectors
        zf[16:32, lanes(i)] = obs_v[pl.ds(i, 1), :] * vectors
        return carry

    lax.fori_loop(0, NB, prepare_own, 0)

    def tiles(b, start, stop, mask):
        count = stop - start
        here = pl.ds(pl.multiple_of((b + start - W) * OBS, OBS), count * OBS)
        every = jnp.dot(lhsx[here, :], rhs[b], preferred_element_type=F32)
        for j in range(start, stop):
            both = every[(j - start) * OBS : (j - start + 1) * OBS]
            shared = both[:, 0:128]
            square = both[:, 128:256]
            inverse = lax.rsqrt(jnp.maximum(square, 1e-30))
            value = jnp.exp2(square * C_CORR * inverse) + jnp.exp2(square * C_LOC) * shared
            hi, lo = split(value * mask(b, j))
            kmat[b, j * OBS : (j + 1) * OBS, 0:128] = hi
            kmat[b, j * OBS : (j + 1) * OBS, 128:256] = lo

    def own_mask(b, j):
        return maskx[j + W, pl.ds(b - W, 1), :]

    def low_mask(b, j):
        return maskx[W - j, b + j - W : b + j - W + 1, :]

    def add(row, place, count, part):
        part = part[0:16] + part[16:32]
        zf[row : row + 16, lanes(place - W, count)] += part * STATIC_VAR

    def gather(b, start, stop, row):
        vectors = zx[row : row + 32, lanes(b + start, stop - start)]
        if row and start == 0:
            vectors = half_first(vectors)
        part = jnp.dot(
            vectors, kmat[b, start * OBS : stop * OBS, :],
            preferred_element_type=F32,
        )
        add(row // 2 + 16, b, 1, part[:, 0:128] + part[:, 128:256])

    def scatter(b, start, stop, row):
        vectors = zx[row : row + 32, lanes(b)]
        part = lax.dot_general(
            jnp.concatenate([vectors, vectors], axis=1), kmat[b, start * OBS : stop * OBS, :],
            (((1,), (1,)), ((), ())), preferred_element_type=F32,
        )
        if row and start == 0:
            part = half_first(part)
        add(row // 2 + 16, b + start, stop - start, part)

    last = NB

    def apply_to(b, inside):
        gather(b, 0, inside, 0)
        if inside > 1:
            scatter(b, 1, inside, 0)

    def step(b, carry):
        apply_to(b - 1, HALF)
        tiles(b, 0, HALF, own_mask)
        return carry

    tiles(W, 0, HALF, own_mask)
    lax.fori_loop(W + 1, 2 * W + 1, step, 0)
    edge_lo[...] = zf[16:32, 0 : W * OBS]
    to_left = remote(edge_lo, p_hi, 12, left)
    to_left.start()
    lax.fori_loop(2 * W + 1, 2 * W + EARLY, step, 0)
    tiles(last - W, W, HALF, own_mask)
    apply_to(2 * W + EARLY - 1, HALF)
    for b in range(last - W + 1, last):
        tiles(b, last - b, HALF, own_mask)
        scatter(b - 1, last + 1 - b, HALF, 0)
    tiles(last, 0, W, own_mask)
    scatter(last - 1, 1, HALF, 0)
    for b in range(last + 1, last + W):
        tiles(b, 0, last + W - b, own_mask)
        apply_to(b - 1, last + W + 1 - b)
    apply_to(last + W - 1, 1)

    edge_hi[...] = zf[16:32, (NB - W) * OBS : NB * OBS]
    to_right = remote(edge_hi, p_lo, 13, right)
    to_right.start()

    small[0].wait()
    small[2].wait()
    for q in range(W):
        set_vectors(q, v_lo[q])
    for q in range(W):
        low = W - 1 - q
        blocks[q][0].wait()
        set_right(low, ens_lo[low], crd_lo[low])
        tiles(low, q + 1, HALF, low_mask)
        if q:
            scatter(low + 1, q, HALF, 0)
    scatter(0, W, HALF, 0)

    small[1].wait()
    small[3].wait()
    for q in range(W):
        set_vectors(q + NB + W, v_hi[q])
    for q in range(W):
        high = last + W + q
        blocks[q][1].wait()
        set_left(high, ens_hi[q], crd_hi[q])
        for j in range(q + 1, HALF):
            tiles(high - j, j, j + 1, own_mask)
    for b in range(last, last + W):
        gather(b, last + W - b, HALF, 0)

    tiles(2 * W + EARLY, 0, HALF, own_mask)
    lax.fori_loop(2 * W + EARLY + 1, last - W, step, 0)
    tiles(last - W, 0, W, own_mask)
    apply_to(last - W - 1, HALF)
    for b in range(last - W + 1, last):
        tiles(b, 0, last - b, own_mask)
        gather(b - 1, 0, HALF, 0)
        scatter(b - 1, 1, last + 1 - b, 0)
    gather(last - 1, 0, HALF, 0)

    def renew(row, source, start):
        hi, lo = split(source)
        zx[row : row + 16, start * OBS : start * OBS + source.shape[1]] = hi
        zx[row + 16 : row + 32, start * OBS : start * OBS + source.shape[1]] = lo

    renew(32, zf[16:32, :], W)

    def upper(b):
        zf[32:48, lanes(b - W)] = 0.5 * obs_v[pl.ds(b - W, 1), :] * zf[16:32, lanes(b - W)]
        gather(b, 0, HALF, 32)

    def uppers(i, carry):
        for more in range(UNROLL):
            upper(W + i * UNROLL + more)
        return carry

    lax.fori_loop(0, (last - W) // UNROLL, uppers, 0)
    for b in range(last, last + W):
        upper_lanes = lanes(b - W)
        zf[32:48, upper_lanes] = 0.5 * obs_v[b - W : b - W + 1, :] * zf[16:32, upper_lanes]
        gather(b, 0, last + W - b, 32)
    lane = lax.broadcasted_iota(jnp.int32, (16, OBS), 1)
    lane8 = lax.broadcasted_iota(jnp.int32, (8, OBS), 1)

    def turn(value, by):
        return pltpu.roll(value, by % OBS, 1)

    def product_gram(left_rows, right_rows):
        value = lax.dot_general(left_rows, right_rows, (((1,), (1,)), ((), ())), preferred_element_type=F32)
        height, width = value.shape
        value = jnp.concatenate([value, jnp.zeros((height, OBS - width), F32)], axis=1)
        value = value[0:16] + value[16:32] if height == 32 else value
        return value + turn(value, -16) if height == 32 else value

    own = slice(W * OBS, (W + NB) * OBS)
    renew(64, zf[32:48, :], W)
    of_r = product_gram(zx[0:32, own], zx[0:64, own])
    of_p = product_gram(zx[32:64, own], zx[32:96, own])
    of_h = product_gram(zx[64:96, own], zx[32:64, own])
    place = lane >> 4
    early = jnp.where(
        place == 0, of_r, jnp.where(place == 1, turn(of_p, 16), jnp.where(place == 2, of_r, turn(of_p, 16) + turn(of_h, 48)))
    )
    def across(row):
        sums = [None] * W
        for b in range(last, last + W):
            start = last + W - b
            vectors = zx[row : row + 32, b * OBS : (b + 1) * OBS]
            part = lax.dot_general(
                jnp.concatenate([vectors, vectors], axis=1), kmat[b, start * OBS :, :],
                (((1,), (1,)), ((), ())), preferred_element_type=F32,
            )
            part = (part[0:16] + part[16:32]) * STATIC_VAR
            for i in range(HALF - start):
                piece = part[:, i * OBS : (i + 1) * OBS]
                sums[i] = piece if sums[i] is None else sums[i] + piece
        return jnp.concatenate(sums, axis=1)

    ours = jnp.concatenate(split(across(32)), axis=0)
    given = across(0)
    to_left.wait()
    upper_halo = p_hi[...] + given
    theirs = jnp.concatenate(split(upper_halo), axis=0)
    late = product_gram(ours, theirs) + product_gram(theirs, ours)
    own_part = jnp.where(place == 3, early + turn(late, 48), early)
    part_a[...] = jnp.where(lane8 < 64, own_part[0:8], turn(own_part[8:16], 64))

    def exchange(part, red, peers, send, recv):
        copies = [
            pltpu.make_async_remote_copy(
                src_ref=part, dst_ref=red.at[i], send_sem=send.at[i], recv_sem=recv.at[i],
                device_id=there, device_id_type=MESH,
            )
            for i, there in enumerate(peers)
        ]
        for copy in copies:
            copy.start()
        return copies

    first_sum = exchange(part_a, red_a, peers_a, send_a, recv_a)

    def rest(i, carry):
        for more in range(UNROLL):
            scatter(W + i * UNROLL + more, 0, HALF, 32)
        return carry

    renew(32, upper_halo, NB + W)
    for b in range(last, last + W):
        gather(b, last + W - b, HALF, 32)
    to_right.wait()
    lower_halo = []
    for b in range(W):
        part = jnp.dot(
            zx[0:32, W * OBS : (b + HALF) * OBS], kmat[b, (W - b) * OBS :, :], preferred_element_type=F32
        )
        part = part[0:16] + part[16:32]
        part = (part[:, 0:128] + part[:, 128:256]) * STATIC_VAR
        lower_halo.append(p_lo[:, b * OBS : (b + 1) * OBS] + part)
    renew(32, jnp.concatenate(lower_halo, axis=1), 0)
    for b in range(W):
        scatter(b, W - b, HALF, 32)
    lax.fori_loop(0, (last - W) // UNROLL, rest, 0)
    for b in range(last, last + W):
        scatter(b, 0, last + W - b, 32)

    def other_half(i, carry):
        zf[32:48, lanes(i)] += 0.5 * obs_v[pl.ds(i, 1), :] * zf[16:32, lanes(i)]
        return carry

    lax.fori_loop(0, NB, other_half, 0)
    for copy in first_sum:
        copy.wait_recv()
    part_b[...] = part_a[...] + jnp.sum(red_a[...], axis=0)
    second_sum = exchange(part_b, red_b, peers_b, send_b, recv_b)
    for copy in first_sum:
        copy.wait_send()
    for copy in second_sum:
        copy.wait_recv()
    packed = part_b[...] + jnp.sum(red_b[...], axis=0)

    moments = jnp.concatenate([packed, turn(packed, 64)], axis=0)
    rows = lax.broadcasted_iota(jnp.int32, (32, OBS), 0)

    lower = turn(moments, -32)
    system = jnp.concatenate([moments, lower], axis=0)
    first_half = [
        jnp.concatenate(
            [
                jnp.broadcast_to(moments[:, 32 + j : 33 + j], (16, OBS)),
                jnp.broadcast_to(moments[:, 16 + j : 17 + j], (16, OBS)),
            ],
            axis=0,
        )
        for j in range(16)
    ]

    def eliminate(spread, system, base):
        inverses = []
        for i in range(16):
            k = base + i
            inverse = 1.0 / spread[i][k : k + 1, :]
            factor = jnp.where(rows == k, 0.0, spread[i] * inverse)
            for j in range(i + 1, 16):
                spread[j] = spread[j] - factor * spread[j][k : k + 1, :]
            system = system - factor * system[k : k + 1, :]
            inverses.append(inverse)
        scaled = system[base : base + 16] * jnp.concatenate(inverses, axis=0)
        return jnp.concatenate([system[0:16], scaled] if base else [scaled, system[16:32]], axis=0)

    system = eliminate(first_half, system, 0)
    second_half = [jnp.broadcast_to(system[:, 16 + j : 17 + j], (32, OBS)) for j in range(16)]
    system = eliminate(second_half, system, 16)

    solved = jnp.concatenate([system, jnp.zeros((96, OBS), F32)], axis=0).T
    for_w = jnp.where(lane < 32, solved[0:16, :], 0.0)
    both = jnp.concatenate([for_w, turn(for_w, 16)], axis=0)[:, 0:48]
    for chunk in range(4):
        here = slice(chunk * 4 * OBS, (chunk + 1) * 4 * OBS)
        sums = jnp.dot(both, zf[:, here], preferred_element_type=F32, precision=lax.Precision.HIGHEST)
        left_over = zf[0:16, here] - sums[16:32]
        for piece in range(4):
            b = chunk * 4 + piece
            w_out[b] = sums[0:16, piece * OBS : (piece + 1) * OBS]
            r_out[b] = left_over[:, piece * OBS : (piece + 1) * OBS]
    for copy in second_sum:
        copy.wait_send()


def on_device(innovations, ensemble, coords, obs_error, pair_cols, pair_count):
    del pair_count
    vmem = pl.BlockSpec(memory_space=pltpu.VMEM)
    arrays = [pltpu.with_memory_space_constraint(a, pltpu.HBM) for a in (innovations, ensemble, coords, obs_error, pair_cols)]
    out = jax.ShapeDtypeStruct((NB, RHS, OBS), F32)
    return pl.pallas_call(
        kernel,
        out_shape=(out, out),
        in_specs=[pl.BlockSpec(memory_space=pltpu.HBM)] * 5,
        out_specs=(vmem, vmem),
        scratch_shapes=[
            pltpu.VMEM((NB, MEM, OBS), F32),
            pltpu.VMEM((NB, 2, OBS), jnp.int32),
            pltpu.VMEM((NB, RHS, OBS), F32),
            pltpu.VMEM((NB, OBS), F32),
            pltpu.VMEM((NB, SLOTS), jnp.int32),
            pltpu.VMEM(((NB + W) * OBS, 256), BF16),
            pltpu.VMEM((NB + W, 256, 256), BF16),
            pltpu.VMEM((NB + W, HALF * OBS, 256), BF16),
            pltpu.VMEM((96, NX * OBS), BF16),
            pltpu.VMEM((48, NB * OBS), F32),
            pltpu.VMEM((SLOTS, NB, OBS), F32),
            pltpu.VMEM((W, MEM, OBS), F32),
            pltpu.VMEM((W, MEM, OBS), F32),
            pltpu.VMEM((W, 2, OBS), jnp.int32),
            pltpu.VMEM((W, 2, OBS), jnp.int32),
            pltpu.VMEM((W, RHS, OBS), F32),
            pltpu.VMEM((W, RHS, OBS), F32),
            pltpu.VMEM((RHS, W * OBS), F32),
            pltpu.VMEM((RHS, W * OBS), F32),
            pltpu.VMEM((RHS, W * OBS), F32),
            pltpu.VMEM((RHS, W * OBS), F32),
            pltpu.VMEM((8, OBS), F32),
            pltpu.VMEM((8, OBS), F32),
            pltpu.VMEM((15, 8, OBS), F32),
            pltpu.VMEM((15, 8, OBS), F32),
            pltpu.SemaphoreType.DMA((5,)),
            pltpu.SemaphoreType.DMA((14,)),
            pltpu.SemaphoreType.DMA((14,)),
            pltpu.SemaphoreType.DMA((15,)),
            pltpu.SemaphoreType.DMA((15,)),
            pltpu.SemaphoreType.DMA((15,)),
            pltpu.SemaphoreType.DMA((15,)),
        ],
        compiler_params=pltpu.CompilerParams(
            collective_id=0, has_side_effects=True, vmem_limit_bytes=LIMIT
        ),
    )(*arrays)


def solution(mesh):
    both = ("region", "sub")
    in_specs = (
        P(both, None, None),
        P(both, None, None),
        P(both, None, None),
        P(both, None),
        P(both, None),
        P(both),
    )
    out_specs = (P(both, None, None), P(both, None, None))
    return jax.shard_map(on_device, mesh=mesh, in_specs=in_specs, out_specs=out_specs, check_vma=False)
```
